256 devices in a mesh: dp: 8 (over y, x_lo), ctx: 16 (over z, x_hi), tp: 2 (over core).
Axes of the slice: x: 4 (x_hi: 2, x_lo: 2; x = x_hi * 2 + x_lo), y: 4, z: 8, core: 2. Of those that a mesh axis runs over, the one named last changes fastest.
Arguments:
- layer_input: bfloat16 [8, 2048, 8192], P('dp', 'ctx'), may hold values from -6 to 6
- queries: bfloat16 [8, 2048, 4096], P('dp', 'ctx', 'tp'), may hold values from -8 to 8
- keys_values: bfloat16 [2, 8, 2048, 512], P(None, 'dp', 'ctx', 'tp'), may hold values from -8 to 8
- grad_attended: bfloat16 [8, 2048, 4096], P('dp', 'ctx', 'tp'), may hold values from -6 to 6
- grad_layer: bfloat16 [8, 2048, 8192], P('dp', 'ctx'), may hold values from -6 to 6
- block_docs: int32 [8, 16], P('dp'), may hold values from 0 to 3, never falling along the last dimension, each value on 1 to 10 neighbouring positions
- wide_candidates: bfloat16 [2, 8, 4096, 256], P(None, 'dp'), may hold values from -3600 to 3600
- narrow_candidates: bfloat16 [2, 8, 512, 256], P(None, 'dp'), may hold values from -3600 to 3600
- proj_owner: int32 [4], replicated, may hold values from 0 to 7
Outputs:
- attended: bfloat16 [8, 2048, 4096], P('dp', 'ctx', 'tp')
- grad_queries: bfloat16 [8, 2048, 4096], P('dp', 'ctx', 'tp')
- grad_keys_values: bfloat16 [2, 8, 2048, 512], P(None, 'dp', 'ctx', 'tp')
- projected_grads: float32 [8192, 4, 256], P(('dp', 'ctx'), None, 'tp')
The draws below stay inside these ranges and needn't reach their ends.
Inputs may be any that keep to these rules, and one draw needn't show every extreme that they name: `block_docs`: along each replica's 16 blocks the ids never fall; each document covers 1 to 10 blocks, and one covers exactly 10. `proj_owner`: entries are for the query, key, value and output projections in that order.
All inputs are finite; a program needn't handle non-finite values.
Results may differ from the reference program's by a relative error of at most 0.027.
Values may be sent and summed in bfloat16 or wider, within the bound.
A program may use at most 128 MiB of HBM per device.

```python
import math
import jax
import jax.numpy as jnp
import numpy as np
from jax import lax

D = 8192
QUERY_HEADS = 32
KEY_VALUE_HEADS = 4
HEAD_SIZE = 128
R = 256
MASK_BLOCK = 128
REPLICA_SEQUENCES = 8
SEQUENCE_TOKENS = 2048
ALLTOK = 16384
NBLK = 16
QW = 4096
KW = 512
DOCS = 4
LONGEST = 10


def draw_queries(key, part):
    key = jax.random.fold_in(key, 11)
    gaussian_part = jax.random.normal(key, (REPLICA_SEQUENCES, SEQUENCE_TOKENS, QUERY_HEADS, HEAD_SIZE), jnp.float32)
    return jnp.clip(gaussian_part, -8.0, 8.0).reshape(REPLICA_SEQUENCES, SEQUENCE_TOKENS, QUERY_HEADS * HEAD_SIZE).astype(jnp.bfloat16)


def draw_keys_values(key, part):
    key = jax.random.fold_in(key, 12)
    gaussian_part = jax.random.normal(key, (2, REPLICA_SEQUENCES, SEQUENCE_TOKENS, KEY_VALUE_HEADS, HEAD_SIZE), jnp.float32)
    return jnp.clip(gaussian_part, -8.0, 8.0).reshape(2, REPLICA_SEQUENCES, SEQUENCE_TOKENS, KEY_VALUE_HEADS * HEAD_SIZE).astype(jnp.bfloat16)


def broad_candidates(key, height, row_top):
    noise_key, row_key, col_key = jax.random.split(key, 3)
    noise_part = jnp.clip(jax.random.normal(noise_key, (2, REPLICA_SEQUENCES, height, R), jnp.float32), -6.0, 6.0)
    row_scale = jnp.exp(jax.random.uniform(row_key, (2, REPLICA_SEQUENCES, height, 1), jnp.float32) * math.log(row_top))
    col_scale = jnp.exp(jax.random.uniform(col_key, (2, REPLICA_SEQUENCES, 1, R), jnp.float32) * math.log(10.0))
    return (noise_part * row_scale * col_scale).astype(jnp.bfloat16)


def draw_wide_candidates(key, part):
    key = jax.random.fold_in(key, 21)
    return broad_candidates(key, QUERY_HEADS * HEAD_SIZE, 10.0)


def draw_narrow_candidates(key, part):
    key = jax.random.fold_in(key, 22)
    return broad_candidates(key, KEY_VALUE_HEADS * HEAD_SIZE, 10.0)


def plant(array, rng, low, largest):
    spot = [jax.random.randint(jax.random.fold_in(rng, axis), (), 0, length) for axis, length in enumerate(array.shape)]
    widest = array.shape.index(max(array.shape))
    next_to = spot[:widest] + [(spot[widest] + 1) % array.shape[widest]] + spot[widest + 1:]
    return array.at[tuple(spot)].set(low).at[tuple(next_to)].set(largest)


def block_levels(rng, shape, cuts, low, top_value):
    def one(axis_at, shards_of):
        heights = jax.random.uniform(jax.random.fold_in(jax.random.fold_in(rng, 6), axis_at), (shards_of,), jnp.float32, low / len(cuts), top_value / len(cuts))
        return jnp.repeat(jnp.exp(heights), shape[axis_at] // shards_of).reshape((-1,) + (1,) * (len(shape) - axis_at - 1))

    loudness = one(*cuts[0])
    for cut in cuts[1:]:
        loudness = loudness * one(*cut)
    return loudness


def split_up(number_of, total, reach, lean):
    portions = [(1 << 20) // math.isqrt(rank ** lean) + 1 for rank in range(2, number_of + 1)]
    spare, holding = total - reach - (number_of - 1), [1] * (number_of - 1)
    while spare > 0:
        candidates = [i for i in range(number_of - 1) if holding[i] < reach]
        pool, budget = sum([portions[i] for i in candidates]), spare
        for i in candidates:
            addition = min(reach - holding[i], max(1, budget * portions[i] // pool), spare)
            holding[i] = holding[i] + addition
            spare = spare - addition
    return np.array([reach] + holding)


def uneven_parts(stream_key, amount, total, bound, lean):
    if amount == 2:
        one = jax.random.randint(stream_key, (), max(1, total - bound), min(bound, total - 1) + 1)
        return jnp.stack([one, total - one])
    lengths = jnp.asarray(split_up(amount, total, bound, lean), jnp.int32)
    couples = (amount - 1) // 2
    source_of, receiver = lengths[1:1 + 2 * couples:2], lengths[2:2 + 2 * couples:2]
    margin = jnp.minimum(source_of - 1, bound - receiver)
    shifted = jax.random.randint(jax.random.fold_in(stream_key, 1), (couples,), 0, 1 << 20) % (margin + 1)
    lengths = lengths.at[1:1 + 2 * couples:2].set(source_of - shifted).at[2:2 + 2 * couples:2].set(receiver + shifted)
    return lengths[jax.random.permutation(jax.random.fold_in(stream_key, 2), amount)]


def scatter_about(key, shape, scale, limit, cuts=(), kind=jnp.bfloat16):
    entries = jax.random.normal(key, shape, jnp.float32) * scale
    if len(cuts) > 0:
        entries = block_levels(key, shape, cuts, -0.22, 0.18) * entries
    return jnp.clip(entries, min=-limit, max=limit).astype(kind)


def setup_inputs(seed: int = 0) -> dict:
    splits = jax.random.split(jax.random.key(seed), 10)
    layer_input = scatter_about(splits[0], (REPLICA_SEQUENCES, SEQUENCE_TOKENS, D), 1.0, 6.0, ((0, 8), (1, 16)))
    queries = draw_queries(jax.random.fold_in(splits[9], 71), 0)
    keys_values = draw_keys_values(jax.random.fold_in(splits[9], 71), 0)
    grad_attended = scatter_about(splits[3], (REPLICA_SEQUENCES, SEQUENCE_TOKENS, QW), 1.0, 6.0, ((0, 8), (1, 16), (2, 2)))
    grad_layer = scatter_about(splits[4], (REPLICA_SEQUENCES, SEQUENCE_TOKENS, D), 1.0, 6.0, ((0, 8), (1, 16)))
    block_docs = jax.vmap(lambda own: jnp.searchsorted(jnp.cumsum(uneven_parts(own, DOCS, NBLK, LONGEST, 1)), jnp.arange(NBLK), side="right"))(jax.random.split(splits[5], REPLICA_SEQUENCES)).reshape((REPLICA_SEQUENCES, NBLK)).astype(jnp.int32)
    wide_candidates = draw_wide_candidates(jax.random.fold_in(splits[9], 71), 0)
    narrow_candidates = draw_narrow_candidates(jax.random.fold_in(splits[9], 71), 0)
    proj_owner = plant(jax.random.randint(splits[8], (4,), 0, REPLICA_SEQUENCES), jax.random.fold_in(splits[8], 1), 0, REPLICA_SEQUENCES - 1).astype(jnp.int32)
    return dict(layer_input=layer_input, queries=queries, keys_values=keys_values, grad_attended=grad_attended, grad_layer=grad_layer, block_docs=block_docs, wide_candidates=wide_candidates, narrow_candidates=narrow_candidates, proj_owner=proj_owner)


def rounded(value):
    return lax.optimization_barrier(value.astype(jnp.bfloat16)).astype(jnp.float32)

def normalize(chosen):
    wide = chosen.astype(jnp.float32)
    return (wide / jnp.sqrt(lax.optimization_barrier(jnp.sum(wide * wide, axis=0)) + 1e-06)).astype(jnp.bfloat16)

def attend_sequence(operands):
    queries, key_rows, value_rows, output_gradient, docs = operands
    group_width = QUERY_HEADS // KEY_VALUE_HEADS
    inv_root = 1.0 / math.sqrt(HEAD_SIZE)
    token_docs = jnp.repeat(docs, MASK_BLOCK)
    positions = jnp.arange(SEQUENCE_TOKENS, dtype=jnp.int32)
    key_head_rows = key_rows.astype(jnp.float32).reshape(SEQUENCE_TOKENS, KEY_VALUE_HEADS, HEAD_SIZE)
    value_head_rows = value_rows.astype(jnp.float32).reshape(SEQUENCE_TOKENS, KEY_VALUE_HEADS, HEAD_SIZE)

    def one_block(kv_grads, block_index):
        leading_row = (block_index * MASK_BLOCK).astype(jnp.int32)
        block_of_queries = lax.dynamic_slice_in_dim(queries, leading_row, MASK_BLOCK, 0).astype(jnp.float32).reshape(MASK_BLOCK, KEY_VALUE_HEADS, group_width, HEAD_SIZE)
        block_gradient = lax.dynamic_slice_in_dim(output_gradient, leading_row, MASK_BLOCK, 0).astype(jnp.float32).reshape(MASK_BLOCK, KEY_VALUE_HEADS, group_width, HEAD_SIZE)
        query_pos = leading_row + jnp.arange(MASK_BLOCK, dtype=jnp.int32)
        query_doc = lax.dynamic_slice_in_dim(token_docs, leading_row, MASK_BLOCK, 0)
        visible_mask = (positions[None, :] <= query_pos[:, None]) & (token_docs[None, :] == query_doc[:, None])
        scores = jnp.einsum('igrd,jgd->grij', block_of_queries, key_head_rows) * inv_root
        scores = jnp.where(visible_mask[None, None], scores, -jnp.inf)
        row_max = lax.optimization_barrier(jnp.max(scores, axis=-1))
        weights = jnp.exp(scores - row_max[..., None])
        row_sum = lax.optimization_barrier(jnp.sum(weights, axis=-1))
        blended = jnp.einsum('grij,jgd->igrd', rounded(weights), value_head_rows)
        attended_block = rounded(blended / jnp.transpose(row_sum, (2, 0, 1))[..., None])
        log_total = row_max + jnp.log(row_sum)
        row_delta = jnp.transpose(lax.optimization_barrier(jnp.sum(block_gradient * attended_block, axis=-1)), (1, 2, 0))
        probs = jnp.exp(scores - log_total[..., None])
        grad_probs = jnp.einsum('igrd,jgd->grij', block_gradient, value_head_rows)
        score_gradient = rounded(probs * (grad_probs - row_delta[..., None]))
        query_grads = (jnp.einsum('grij,jgd->igrd', score_gradient, key_head_rows) * inv_root).astype(jnp.bfloat16)
        key_grads = jnp.einsum('grij,igrd->jgd', score_gradient, block_of_queries) * inv_root
        value_grads = jnp.einsum('grij,igrd->jgd', rounded(probs), block_gradient)
        outputs = (attended_block.astype(jnp.bfloat16).reshape(MASK_BLOCK, QW), query_grads.reshape(MASK_BLOCK, QW))
        return ((kv_grads[0] + key_grads, kv_grads[1] + value_grads), outputs)
    empty_block = jnp.zeros((SEQUENCE_TOKENS, KEY_VALUE_HEADS, HEAD_SIZE), jnp.float32)
    (key_total, value_total), (attended_rows, query_rows) = lax.scan(one_block, (empty_block, empty_block), jnp.arange(NBLK, dtype=jnp.int32))
    return (attended_rows.reshape(SEQUENCE_TOKENS, QW), query_rows.reshape(SEQUENCE_TOKENS, QW), key_total.reshape(SEQUENCE_TOKENS, KW).astype(jnp.bfloat16), value_total.reshape(SEQUENCE_TOKENS, KW).astype(jnp.bfloat16))

def reference(layer_input, queries, keys_values, grad_attended, grad_layer, block_docs, wide_candidates, narrow_candidates, proj_owner):
    attended, grad_queries, grad_keys, grad_values = lax.map(attend_sequence, (queries, keys_values[0], keys_values[1], grad_attended, block_docs))
    basis_query = normalize(lax.dynamic_index_in_dim(wide_candidates[0], proj_owner[0], 0, keepdims=False))
    basis_key = normalize(lax.dynamic_index_in_dim(narrow_candidates[0], proj_owner[1], 0, keepdims=False))
    basis_value = normalize(lax.dynamic_index_in_dim(narrow_candidates[1], proj_owner[2], 0, keepdims=False))
    basis_output = normalize(lax.dynamic_index_in_dim(wide_candidates[1], proj_owner[3], 0, keepdims=False))

    def moment(data, basis):
        width = data.shape[-1]
        flat = jnp.dot(data.reshape(REPLICA_SEQUENCES * SEQUENCE_TOKENS, width), basis, preferred_element_type=jnp.float32)
        return flat.reshape(REPLICA_SEQUENCES, SEQUENCE_TOKENS, R)
    moments = jnp.stack([moment(grad_queries, basis_query), moment(grad_keys, basis_key), moment(grad_values, basis_value), moment(attended, basis_output)], axis=2).astype(jnp.bfloat16)

    def add_replica(summed, replica):
        inputs = layer_input[replica]
        upstream = grad_layer[replica]
        parts = moments[replica]
        triple = jnp.dot(inputs.T, parts[:, :3].reshape(SEQUENCE_TOKENS, 3 * R), preferred_element_type=jnp.float32).reshape(D, 3, R)
        single = jnp.dot(upstream.T, parts[:, 3], preferred_element_type=jnp.float32)
        return (summed + jnp.concatenate([triple, single[:, None]], axis=1), None)
    summed, unused = lax.scan(add_replica, jnp.zeros((D, 4, R), jnp.float32), jnp.arange(REPLICA_SEQUENCES, dtype=jnp.int32))
    projected_grads = summed / math.sqrt(ALLTOK)
    grad_keys_values = jnp.stack([grad_keys, grad_values], axis=0)
    return (attended, grad_queries, grad_keys_values, projected_grads)
```

```python
import math

import jax
import jax.numpy as jnp
from jax import lax
from jax.experimental import pallas as pl
from jax.experimental.pallas import tpu as pltpu
from jax.sharding import PartitionSpec as P

HEAD = 128
BLOCK = 128
LONGEST = 10
NEG = -1e30
MESH = pl.DeviceIdType.MESH
BF16 = jnp.bfloat16
F32 = jnp.float32
INV_ROOT = 1.0 / math.sqrt(HEAD)

NX = 2
NY = 4
NZ = 8
PLANE = NX * NX * NY


def dot(a, b, dims=((1,), (0,))):
    return lax.dot_general(a, b, (dims, ((), ())), preferred_element_type=F32)


def kernel(
    x_ref, q_ref, kv_ref, do_ref, gl_ref, docs_ref, wide_ref, narrow_ref, owner_ref,
    att_out, gq_out, gkv_out, proj_out,
    qf, dof, qs, dos, qt, dot_, kvg, w, mx, den, delta, ot, dqt, attf, gqf,
    dsend, dacc, xrecv, tin, ext, kvo,
    bxw, bxn, byw, byn, basw, basn, xr, xt, pm, sx, rx, mm, rs, rr, ssq, rssq,
    load_sem, out_sem,
    kv_recv, kv_send_z, kv_send_x, kv_send_9,
    x_send, x_recv, t_send, t_recv, ext_send, ext_recv,
    bx_send, bx_recv, by_send, by_recv, ring_send, ring_recv,
    a_send, a_recv, sib_send, sib_recv, m_send, m_recv, r_send, r_recv,
):
    d = lax.axis_index("dp")
    c = lax.axis_index("ctx")
    t = lax.axis_index("tp")
    y, xl = lax.div(d, NX), lax.rem(d, NX)
    z, xh = lax.div(c, NX), lax.rem(c, NX)
    plane = d * NX + xh
    partner = (d, c + 1 - 2 * xh, t)
    above = (d, c + NX, t)
    below = (d, c - NX, t)
    sibling = (d, c, 1 - t)

    def local(src, dst, sem):
        return pltpu.make_async_copy(src, dst, sem)

    def remote(src, dst, send, recv, device):
        return pltpu.make_async_remote_copy(
            src_ref=src, dst_ref=dst, send_sem=send, recv_sem=recv,
            device_id=device, device_id_type=MESH,
        )

    def arrived(dst, recv):
        remote(dst, dst, recv, recv, sibling).wait_recv()

    def left(src, send):
        remote(src, src, send, send, sibling).wait_send()

    def loop(low, high, body):
        def step(i, carry):
            body(i)
            return carry
        lax.fori_loop(low, high, step, 0)

    q_load = local(q_ref.at[0], qf, load_sem.at[0])
    do_load = local(do_ref.at[0], dof, load_sem.at[1])
    kv_load = local(kv_ref.at[:, 0], kvg.at[0], load_sem.at[2])
    wide_mine = wide_ref.at[:, 0, pl.ds(pl.multiple_of(t * 2048 + z * 256, 256), 256), :]
    narrow_mine = narrow_ref.at[:, 0, pl.ds(pl.multiple_of(t * 256 + z * 32, 32), 32), :]
    w_load = local(wide_mine, bxw.at[xl], load_sem.at[3])
    n_load = local(narrow_mine, bxn.at[xl], load_sem.at[4])
    kv_load.start()
    q_load.start()
    do_load.start()
    w_load.start()
    n_load.start()

    barrier = pltpu.get_barrier_semaphore()

    def greet(device):
        pl.semaphore_signal(barrier, inc=1, device_id=device, device_id_type=MESH)

    def plane_device(k):
        other = lax.rem(plane + k, PLANE)
        return other, (lax.div(other, NX), z * NX + lax.rem(other, NX), t)

    loop(1, PLANE, lambda k: greet(plane_device(k)[1]))

    def greet_column(k):
        zz = lax.rem(z + k, NZ)
        greet((d, zz * NX, t))
        greet((d, zz * NX + 1, t))

    loop(1, NZ, greet_column)
    greet(sibling)
    pl.semaphore_wait(barrier, (PLANE - 1) + 2 * (NZ - 1) + 1)

    def forward_kv(s):
        slot = 2 * s

        @pl.when((s <= 3) & (z <= NZ - 2))
        def _():
            remote(kvg.at[slot], kvg.at[slot + 2], kv_send_z.at[s], kv_recv.at[slot + 2], above).start()

        @pl.when(xh == 0)
        def _():
            remote(kvg.at[slot], kvg.at[slot + 1], kv_send_x.at[s], kv_recv.at[slot + 1], partner).start()

        @pl.when((xh == 1) & (s >= 1))
        def _():
            remote(kvg.at[slot], kvg.at[slot - 1], kv_send_x.at[s], kv_recv.at[slot - 1], partner).start()

        @pl.when((xh == 1) & (s == 4) & (z <= NZ - 2))
        def _():
            remote(kvg.at[8], kvg.at[9], kv_send_9.at[0], kv_recv.at[9], (d, c + 1, t)).start()

    kv_load.wait()
    forward_kv(0)

    across = (d + 1 - 2 * xl, c, t)
    bx_copies = (
        remote(wide_mine, bxw.at[xl], bx_send.at[0], bx_recv.at[0], across),
        remote(narrow_mine, bxn.at[xl], bx_send.at[1], bx_recv.at[1], across),
    )
    for copy in bx_copies:
        copy.start()

    q_load.wait()
    do_load.wait()

    def split_heads(h):
        g, i = lax.div(h, 8), lax.rem(h, 8)
        columns = pl.ds(pl.multiple_of(h * HEAD, HEAD), HEAD)
        rows = pl.ds(pl.multiple_of(i * HEAD, HEAD), HEAD)
        tile = qf[:, columns]
        qs[g, rows, :] = tile
        qt[g, :, rows] = tile.T
        tile = dof[:, columns]
        dos[g, rows, :] = tile
        dot_[g, :, rows] = tile.T

    loop(0, 16, split_heads)

    def score(j, diagonal=False):
        if not diagonal:
            same = docs_ref[0, c] == docs_ref[0, c - j]
            bias = jnp.where(same, 0.0, NEG).astype(F32)
        for g in range(2):
            key = kvg[j, 0, :, g * HEAD:(g + 1) * HEAD]
            s = dot(key, qt[g]) * INV_ROOT
            if diagonal:
                rows = lax.broadcasted_iota(jnp.int32, s.shape, 0)
                lanes = lax.broadcasted_iota(jnp.int32, s.shape, 1) & (BLOCK - 1)
                s = jnp.where(rows <= lanes, s, NEG)
                mx[g] = jnp.max(s, axis=0, keepdims=True)
            else:
                s = s + bias
                mx[g] = jnp.maximum(mx[g], jnp.max(s, axis=0, keepdims=True))
            w[j, g] = s

    score(0, True)

    def forward_step(s):
        @pl.when(z >= s)
        def _():
            arrived(kvg.at[2 * s], kv_recv.at[2 * s])
            forward_kv(s)
            score(2 * s)

        @pl.when(z + xh >= s)
        def _():
            arrived(kvg.at[2 * s - 1], kv_recv.at[2 * s - 1])
            score(2 * s - 1)

    loop(1, 3, forward_step)

    for copy in bx_copies:
        copy.wait_recv()
    w_load.wait()
    n_load.wait()
    owners = [owner_ref[m] for m in range(4)]
    for m, n in ((0, 0), (1, 3)):
        byw[y, m] = bxw[lax.rem(owners[n], NX), m]
    for m, n in ((0, 1), (1, 2)):
        byn[y, m] = bxn[lax.rem(owners[n], NX), m]

    def y_copies(k):
        device = (lax.rem(y + k, NY) * NX + xl, c, t)
        return (
            remote(byw.at[y], byw.at[y], by_send.at[k, 0], by_recv.at[y, 0], device),
            remote(byn.at[y], byn.at[y], by_send.at[k, 1], by_recv.at[y, 1], device),
        )

    for k in range(1, NY):
        for copy in y_copies(k):
            copy.start()

    loop(3, 5, forward_step)

    @pl.when(z + xh >= 5)
    def _():
        arrived(kvg.at[9], kv_recv.at[9])
        score(9)

    def a_copy(source, k):
        other, device = plane_device(k)
        columns = pl.ds(pl.multiple_of(other * 512, 512), 512)
        return remote(source.at[0, :, columns], xr.at[t, plane], a_send.at[k], a_recv.at[plane], device)

    mine = pl.ds(pl.multiple_of(plane * 512, 512), 512)

    @pl.when(t == 0)
    def _():
        loop(1, PLANE, lambda k: a_copy(x_ref, k).start())
        local(x_ref.at[0, :, mine], xr.at[0, plane], load_sem.at[5]).start()

    @pl.when(t == 1)
    def _():
        loop(1, PLANE, lambda k: a_copy(gl_ref, k).start())
        local(gl_ref.at[0, :, mine], xr.at[1, plane], load_sem.at[5]).start()

    def y_arrived(k):
        yy = lax.rem(y + k, NY)
        arrived(byw.at[yy], by_recv.at[yy, 0])
        arrived(byn.at[yy], by_recv.at[yy, 1])

    for k in range(1, NY):
        y_arrived(k)
    for m, n in ((0, 0), (1, 3)):
        basw[m, pl.ds(pl.multiple_of(z * 256, 256), 256), :] = byw[lax.div(owners[n], NX), m]
    for m, n in ((0, 1), (1, 2)):
        basn[m, pl.ds(pl.multiple_of(z * 32, 32), 32), :] = byn[lax.div(owners[n], NX), m]

    z_up = (d, lax.rem(z + 1, NZ) * NX + xh, t)
    z_down = (d, lax.rem(z + NZ - 1, NZ) * NX + xh, t)

    def eighth(p):
        p = lax.rem(p + 2 * NZ, NZ)
        return (
            basw.at[:, pl.ds(pl.multiple_of(p * 256, 256), 256), :],
            basn.at[:, pl.ds(pl.multiple_of(p * 32, 32), 32), :],
        )

    def ring_copies(k):
        copies = []
        for way, device, p in ((0, z_up, z - k), (1, z_down, z + k)):
            if way == 1 and k == 3:
                continue
            for n, ref in enumerate(eighth(p)):
                copies.append(remote(ref, ref, ring_send.at[way, k, n], ring_recv.at[way, k, n], device))
        return copies

    def ring_arrived(k):
        for way, p in ((0, z - 1 - k), (1, z + 1 + k)):
            if way == 1 and k == 3:
                continue
            for n, ref in enumerate(eighth(p)):
                arrived(ref, ring_recv.at[way, k, n])

    def ring_step(k):
        if k >= 1:
            ring_arrived(k - 1)
        if k <= 3:
            for copy in ring_copies(k):
                copy.start()

    ring_step(0)

    den[...] = jnp.zeros_like(den)
    ot[...] = jnp.zeros_like(ot)
    dqt[...] = jnp.zeros_like(dqt)

    def weigh(j):
        for g in range(2):
            value = kvg[j, 1, :, g * HEAD:(g + 1) * HEAD]
            p = jnp.exp(w[j, g] - mx[g])
            w[j, g] = p
            den[g] += jnp.sum(p, axis=0, keepdims=True)
            ot[g] += dot(value, p.astype(BF16), ((0,), (0,)))

    loop(0, jnp.minimum(c, LONGEST - 1) + 1, weigh)
    for g in range(2):
        den[g] = 1.0 / den[g]

    def finish_heads(h):
        g, i = lax.div(h, 8), lax.rem(h, 8)
        columns = pl.ds(pl.multiple_of(h * HEAD, HEAD), HEAD)
        rows = pl.ds(pl.multiple_of(i * HEAD, HEAD), HEAD)
        low = (ot[g, :, rows] * den[g, :, rows]).astype(BF16).astype(F32)
        delta[g, :, rows] = jnp.sum(low * dot_[g, :, rows].astype(F32), axis=0, keepdims=True)
        attf[:, columns] = low.T.astype(BF16)

    loop(0, 16, finish_heads)
    att_store = local(attf, att_out.at[0], out_sem.at[0])
    att_store.start()
    ring_step(1)

    def backward(j, store):
        for g in range(2):
            columns = slice(g * HEAD, (g + 1) * HEAD)
            key = kvg[j, 0, :, columns]
            value = kvg[j, 1, :, columns]
            p = w[j, g] * den[g]
            ds = (p * (dot(value, dot_[g]) - delta[g])).astype(BF16)
            dqt[g] += dot(key, ds, ((0,), (0,)))
            store(0, columns, dot(ds, qs[g]) * INV_ROOT)
            store(1, columns, dot(p.astype(BF16), dos[g]))

    def chain(s):
        @pl.when(z >= s)
        def _():
            @pl.when((xh == 0) | (s >= 1))
            def _():
                arrived(xrecv.at[s], x_recv.at[s])
                dacc[s] += xrecv[s].astype(F32)

            @pl.when((s == 4) & (xh == 1) & (z <= NZ - 2))
            def _():
                arrived(ext, ext_recv.at[0])
                dacc[s] += ext[...].astype(F32)

            @pl.when((s <= 3) & (z <= NZ - 2))
            def _():
                arrived(tin.at[s], t_recv.at[s])
                dacc[s] += tin[s].astype(F32)

            @pl.when(s >= 1)
            def _():
                dsend[2 * s] = dacc[s].astype(BF16)
                remote(dsend.at[2 * s], tin.at[s - 1], t_send.at[s], t_recv.at[s - 1], below).start()

    def backward_step(i):
        s = 4 - i

        @pl.when(z + xh >= s + 1)
        def _():
            def store(which, columns, val):
                dsend[2 * s + 1, which, :, columns] = val.astype(BF16)

            backward(2 * s + 1, store)

            @pl.when(xh == 1)
            def _():
                remote(dsend.at[2 * s + 1], xrecv.at[s], x_send.at[s], x_recv.at[s], partner).start()

            @pl.when((xh == 0) & (s <= 3))
            def _():
                remote(dsend.at[2 * s + 1], xrecv.at[s + 1], x_send.at[s], x_recv.at[s + 1], partner).start()

            @pl.when((xh == 0) & (s == 4))
            def _():
                remote(dsend.at[9], ext, ext_send.at[0], ext_recv.at[0], (d, c - 1, t)).start()

        @pl.when(z >= s)
        def _():
            def store(which, columns, val):
                dacc[s, which, :, columns] = val

            backward(2 * s, store)

        @pl.when(i >= 1)
        def _():
            chain(s + 1)

    loop(0, 2, backward_step)
    ring_step(2)
    loop(2, 4, backward_step)
    ring_step(3)
    loop(4, 5, backward_step)

    def finish_grads(h):
        g, i = lax.div(h, 8), lax.rem(h, 8)
        columns = pl.ds(pl.multiple_of(h * HEAD, HEAD), HEAD)
        rows = pl.ds(pl.multiple_of(i * HEAD, HEAD), HEAD)
        gqf[:, columns] = (dqt[g, :, rows] * INV_ROOT).T.astype(BF16)

    loop(0, 16, finish_grads)
    gq_store = local(gqf, gq_out.at[0], out_sem.at[1])
    gq_store.start()

    local(xr.at[t, plane], xr.at[t, plane], load_sem.at[5]).wait()

    def a_arrived(k):
        other = lax.rem(plane + k, PLANE)
        arrived(xr.at[t, other], a_recv.at[other])

    loop(1, PLANE, a_arrived)
    hand_over = remote(xr.at[t], xr.at[t], sib_send.at[0], sib_recv.at[0], sibling)
    hand_over.start()
    ring_step(4)

    low_half = pl.ds(pl.multiple_of(t * 128, 128), 128)
    high_half = pl.ds(pl.multiple_of((1 - t) * 128, 128), 128)

    def give(part, pairs):
        for n, (rows, basis) in enumerate(pairs):
            pm[part, n] = dot(rows, basis)
            sx[part, n] = pm[part, n, :, high_half].astype(BF16)
        copy = remote(sx.at[part], rx.at[part], sib_send.at[1 + part], sib_recv.at[1 + part], sibling)
        copy.start()
        return copy

    def m_copy(part, k):
        ref = mm.at[part, plane]
        return remote(ref, ref, m_send.at[part, k], m_recv.at[part, plane], plane_device(k)[1])

    def spread(part):
        arrived(rx.at[part], sib_recv.at[1 + part])
        for n in range(2):
            share = pm[part, n, :, low_half] + rx[part, n].astype(F32)
            mm[part, plane, :, n * 128:(n + 1) * 128] = share.astype(BF16)
        loop(1, PLANE, lambda k: m_copy(part, k).start())

    give_a = give(0, ((attf[...], basw[1]), (gqf[...], basw[0])))
    for m, (ref, n) in enumerate(((basw, 0), (basn, 0), (basn, 1), (basw, 1))):
        wide = ref[n].astype(F32)
        ssq[m:m + 1, :] = jnp.sum(wide * wide, axis=0, keepdims=True)
    give_s = remote(ssq, rssq, sib_send.at[3], sib_recv.at[3], sibling)
    give_s.start()
    spread(0)

    chain(0)
    kvo[...] = dacc[0].astype(BF16)
    kv_store = local(kvo, gkv_out.at[:, 0], out_sem.at[2])
    kv_store.start()
    give_b = give(1, ((kvo[0], basn[0]), (kvo[1], basn[1])))
    spread(1)

    def turn(a):
        def one(p):
            for n in range(4):
                xt[a, n * 128:(n + 1) * 128, pl.ds(pl.multiple_of(p * 128, 128), 128)] = (
                    xr[a, p, :, n * 128:(n + 1) * 128].T
                )
        loop(0, PLANE, one)

    turn(t)
    arrived(xr.at[1 - t], sib_recv.at[0])
    turn(1 - t)

    def m_arrived(part):
        def one(k):
            other = lax.rem(plane + k, PLANE)
            arrived(mm.at[part, other], m_recv.at[part, other])
        loop(1, PLANE, one)

    def piece_device(k):
        zz = xh * 4 + lax.div(k, 2)
        return zz, lax.rem(k, 2)

    def reduce_out(part):
        def one(k):
            zz, xx = piece_device(k)
            own = (zz == z) & (xx == xh)

            @pl.when(own)
            def _():
                rr[part, z] = rs[part, k]

            @pl.when(jnp.logical_not(own))
            def _():
                remote(
                    rs.at[part, k], rr.at[part, z], r_send.at[part, k], r_recv.at[part, z],
                    (d, zz * NX + xx, t),
                ).start()

        loop(0, 8, one)

    def outer(part):
        m_arrived(part)

        def one(n):
            rows = pl.ds(pl.multiple_of(n * 128, 128), 128)
            if part == 0:
                out = dot(xt[1, rows, :], mm[0, :, :, 0:128].reshape(PLANE * 128, 128))
                gq = dot(xt[0, rows, :], mm[0, :, :, 128:256].reshape(PLANE * 128, 128))
                val = jnp.concatenate([out, gq], axis=1)
            else:
                val = dot(xt[0, rows, :], mm[1].reshape(PLANE * 128, 256))
            rs[part, pl.ds(2 * n, 2)] = val.astype(BF16).reshape(2, 64, 256)

        loop(0, 4, one)
        reduce_out(part)

    outer(0)
    outer(1)

    source = lax.div(z, 4)

    def r_arrived(part):
        def one(zz):
            @pl.when(jnp.logical_not((source == xh) & (zz == z)))
            def _():
                arrived(rr.at[part, zz], r_recv.at[part, zz])
        loop(0, NZ, one)

    arrived(rssq, sib_recv.at[3])
    rssq[...] = lax.rsqrt(ssq[...] + rssq[...] + 1e-06) * (1.0 / 128.0)
    for part, places in ((0, (3, 0)), (1, (1, 2))):
        r_arrived(part)
        total = jnp.sum(rr[part].astype(F32), axis=0)
        for n, m in enumerate(places):
            proj_out[:, m, :] = total[:, n * 128:(n + 1) * 128] * rssq[m:m + 1, low_half]

    att_store.wait()
    gq_store.wait()
    kv_store.wait()

    def kv_left(s):
        @pl.when((z >= s) & (s <= 3) & (z <= NZ - 2))
        def _():
            left(kvg.at[0], kv_send_z.at[s])

        @pl.when((z >= s) & ((xh == 0) | (s >= 1)))
        def _():
            left(kvg.at[0], kv_send_x.at[s])

        @pl.when((z >= s) & (s >= 1))
        def _():
            left(dsend.at[0], t_send.at[s])

        @pl.when((z + xh >= s + 1) & ((xh == 1) | (s <= 3)))
        def _():
            left(dsend.at[0], x_send.at[s])

    loop(0, 5, kv_left)

    @pl.when((xh == 1) & (z >= 4) & (z <= NZ - 2))
    def _():
        left(kvg.at[0], kv_send_9.at[0])

    @pl.when((xh == 0) & (z >= 5))
    def _():
        left(dsend.at[0], ext_send.at[0])

    for copy in bx_copies:
        copy.wait_send()
    for k in range(1, NY):
        for copy in y_copies(k):
            copy.wait_send()
    for k in range(4):
        for copy in ring_copies(k):
            copy.wait_send()

    def plane_left(k):
        left(xr.at[0, 0], a_send.at[k])
        left(mm.at[0, 0], m_send.at[0, k])
        left(mm.at[1, 0], m_send.at[1, k])

    loop(1, PLANE, plane_left)
    for copy in (hand_over, give_a, give_b, give_s):
        copy.wait_send()

    def reduce_left(k):
        zz, xx = piece_device(k)

        @pl.when(jnp.logical_not((zz == z) & (xx == xh)))
        def _():
            left(rs.at[0, 0], r_send.at[0, k])
            left(rs.at[1, 0], r_send.at[1, k])

    loop(0, 8, reduce_left)


def on_device(*args):
    dma = pltpu.SemaphoreType.DMA
    vmem = pltpu.VMEM
    scratch = [
        vmem((128, 2048), BF16), vmem((128, 2048), BF16),
        vmem((2, 1024, 128), BF16), vmem((2, 1024, 128), BF16),
        vmem((2, 128, 1024), BF16), vmem((2, 128, 1024), BF16),
        vmem((LONGEST, 2, 128, 256), BF16),
        vmem((LONGEST, 2, 128, 1024), F32),
        vmem((2, 1, 1024), F32), vmem((2, 1, 1024), F32), vmem((2, 1, 1024), F32),
        vmem((2, 128, 1024), F32), vmem((2, 128, 1024), F32),
        vmem((128, 2048), BF16), vmem((128, 2048), BF16),
        vmem((LONGEST, 2, 128, 256), BF16), vmem((5, 2, 128, 256), F32),
        vmem((5, 2, 128, 256), BF16), vmem((4, 2, 128, 256), BF16),
        vmem((2, 128, 256), BF16), vmem((2, 128, 256), BF16),
        vmem((2, 2, 256, 256), BF16), vmem((2, 2, 32, 256), BF16),
        vmem((4, 2, 256, 256), BF16), vmem((4, 2, 32, 256), BF16),
        vmem((2, 2048, 256), BF16), vmem((2, 256, 256), BF16),
        vmem((2, PLANE, 128, 512), BF16), vmem((2, 512, 2048), BF16),
        vmem((2, 2, 128, 256), F32), vmem((2, 2, 128, 128), BF16), vmem((2, 2, 128, 128), BF16),
        vmem((2, PLANE, 128, 256), BF16),
        vmem((2, 8, 64, 256), BF16), vmem((2, 8, 64, 256), BF16),
        vmem((4, 256), F32), vmem((4, 256), F32),
        dma((6,)), dma((3,)),
        dma((10,)), dma((4,)), dma((5,)), dma((1,)),
        dma((5,)), dma((5,)), dma((5,)), dma((4,)), dma((1,)), dma((1,)),
        dma((2,)), dma((2,)), dma((4, 2)), dma((4, 2)), dma((2, 4, 2)), dma((2, 4, 2)),
        dma((PLANE,)), dma((PLANE,)), dma((4,)), dma((4,)),
        dma((2, PLANE)), dma((2, PLANE)), dma((2, 8)), dma((2, 8)),
    ]
    hbm = pl.BlockSpec(memory_space=pl.ANY)
    smem = pl.BlockSpec(memory_space=pltpu.SMEM)
    return pl.pallas_call(
        kernel,
        out_shape=(
            jax.ShapeDtypeStruct((1, 128, 2048), BF16),
            jax.ShapeDtypeStruct((1, 128, 2048), BF16),
            jax.ShapeDtypeStruct((2, 1, 128, 256), BF16),
            jax.ShapeDtypeStruct((64, 4, 128), F32),
        ),
        in_specs=[hbm] * 5 + [smem] + [hbm] * 2 + [smem],
        out_specs=(hbm, hbm, hbm, pl.BlockSpec(memory_space=pltpu.VMEM)),
        scratch_shapes=scratch,
        compiler_params=pltpu.CompilerParams(
            collective_id=0, has_side_effects=True, vmem_limit_bytes=60 * 1024 * 1024
        ),
        cost_estimate=pl.CostEstimate(flops=7_000_000_000, bytes_accessed=12_000_000, transcendentals=3_000_000),
    )(*args)


def solution(mesh):
    return jax.shard_map(
        on_device,
        mesh=mesh,
        in_specs=(
            P("dp", "ctx", None),
            P("dp", "ctx", "tp"),
            P(None, "dp", "ctx", "tp"),
            P("dp", "ctx", "tp"),
            P("dp", "ctx", None),
            P("dp", None),
            P(None, "dp", None, None),
            P(None, "dp", None, None),
            P(),
        ),
        out_specs=(
            P("dp", "ctx", "tp"),
            P("dp", "ctx", "tp"),
            P(None, "dp", "ctx", "tp"),
            P(("dp", "ctx"), None, "tp"),
        ),
        check_vma=False,
    )
```

```python
import math

import jax
import jax.numpy as jnp
from jax import lax
from jax.experimental import pallas as pl
from jax.experimental.pallas import tpu as pltpu
from jax.sharding import PartitionSpec as P

HEAD = 128
BLOCK = 128
LONGEST = 10
NEG = -1e30
MESH = pl.DeviceIdType.MESH
BF16 = jnp.bfloat16
F32 = jnp.float32
INV_ROOT = 1.0 / math.sqrt(HEAD)

NX = 2
NY = 4
NZ = 8
PLANE = NX * NX * NY


def dot(a, b, dims=((1,), (0,))):
    return lax.dot_general(a, b, (dims, ((), ())), preferred_element_type=F32)


def kernel(
    x_ref, q_ref, kv_ref, do_ref, gl_ref, docs_ref, wide_ref, narrow_ref, owner_ref,
    att_out, gq_out, gkv_out, proj_out,
    qf, dof, qs, dos, qt, dot_, kvg, w, mx, den, delta, ot, dqt,
    dsend, dacc, xrecv, tin, ext,
    bx, pk, by, bas, xr, xt, pm, sx, rx, mm, rs, rr, ssq, rssq,
    load_sem,
    kv_recv, kv_send_z, kv_send_x, kv_send_9,
    x_send, x_recv, t_send, t_recv, ext_send, ext_recv,
    bx_send, bx_recv, by_send, by_recv, ring_send, ring_recv, yf_send, yf_recv,
    a_send, a_recv, sib_send, sib_recv, m_send, m_recv, r_send, r_recv,
):
    d = lax.axis_index("dp")
    c = lax.axis_index("ctx")
    t = lax.axis_index("tp")
    y, xl = lax.div(d, NX), lax.rem(d, NX)
    z, xh = lax.div(c, NX), lax.rem(c, NX)
    plane = d * NX + xh
    odd, odd_z = lax.rem(y, 2), lax.rem(z, 2)
    side = xh + odd_z * (1 - 2 * xh)
    partner = (d, c + 1 - 2 * xh, t)
    above = (d, c + NX, t)
    below = (d, c - NX, t)
    sibling = (d, c, 1 - t)

    def local(src, dst, sem):
        return pltpu.make_async_copy(src, dst, sem)

    def remote(src, dst, send, recv, device):
        return pltpu.make_async_remote_copy(
            src_ref=src, dst_ref=dst, send_sem=send, recv_sem=recv,
            device_id=device, device_id_type=MESH,
        )

    def arrived(dst, recv):
        remote(dst, dst, recv, recv, sibling).wait_recv()

    def left(src, send):
        remote(src, src, send, send, sibling).wait_send()

    def loop(low, high, body):
        def step(i, carry):
            body(i)
            return carry
        lax.fori_loop(low, high, step, 0)

    q_load = local(q_ref.at[0], qf, load_sem.at[0])
    do_load = local(do_ref.at[0], dof, load_sem.at[1])
    kv_load = local(kv_ref.at[:, 0], kvg.at[0], load_sem.at[2])

    def mine_of(half):
        return (
            wide_ref.at[half, 0, pl.ds(pl.multiple_of(t * 2048 + z * 256, 256), 256), :],
            narrow_ref.at[half, 0, pl.ds(pl.multiple_of(t * 256 + z * 32, 32), 32), :],
        )

    b_loads = []
    for half in range(2):
        for n, (source, rows) in enumerate(zip(mine_of(half), (pl.ds(0, 256), pl.ds(256, 32)))):
            b_loads.append(local(source, bx.at[half, xl, rows], load_sem.at[3 + 2 * half + n]))
    kv_load.start()
    q_load.start()
    do_load.start()
    for copy in b_loads:
        copy.start()

    barrier = pltpu.get_barrier_semaphore()

    def greet(device):
        pl.semaphore_signal(barrier, inc=1, device_id=device, device_id_type=MESH)

    def plane_device(k):
        other = lax.rem(plane + k, PLANE)
        return other, (lax.div(other, NX), z * NX + lax.rem(other, NX), t)

    loop(1, PLANE, lambda k: greet(plane_device(k)[1]))

    def greet_column(k):
        zz = lax.rem(z + k, NZ)
        greet((d, zz * NX, t))
        greet((d, zz * NX + 1, t))

    loop(1, NZ, greet_column)
    greet(sibling)

    def split_heads(h):
        g, i = lax.div(h, 8), lax.rem(h, 8)
        columns = pl.ds(pl.multiple_of(h * HEAD, HEAD), HEAD)
        rows = pl.ds(pl.multiple_of(i * HEAD, HEAD), HEAD)
        tile = qf[:, columns]
        qs[g, rows, :] = tile
        qt[g, :, rows] = tile.T
        tile = dof[:, columns]
        dos[g, rows, :] = tile
        dot_[g, :, rows] = tile.T

    q_load.wait()
    do_load.wait()
    loop(0, 16, split_heads)
    kv_load.wait()

    def score(j, diagonal=False):
        if not diagonal:
            same = docs_ref[0, c] == docs_ref[0, c - j]
            bias = jnp.where(same, 0.0, NEG).astype(F32)
        for g in range(2):
            key = kvg[j, 0, :, g * HEAD:(g + 1) * HEAD]
            s = dot(key, qt[g]) * INV_ROOT
            if diagonal:
                rows = lax.broadcasted_iota(jnp.int32, s.shape, 0)
                lanes = lax.broadcasted_iota(jnp.int32, s.shape, 1) & (BLOCK - 1)
                s = jnp.where(rows <= lanes, s, NEG)
                mx[g] = jnp.max(s, axis=0, keepdims=True)
            else:
                s = s + bias
                mx[g] = jnp.maximum(mx[g], jnp.max(s, axis=0, keepdims=True))
            w[j, g] = s

    score(0, True)
    pl.semaphore_wait(barrier, (PLANE - 1) + 2 * (NZ - 1) + 1)

    def forward_kv(s, h):
        slot = 2 * s

        def to(dst, send, device):
            remote(kvg.at[slot, h], kvg.at[dst, h], send, kv_recv.at[dst, h], device).start()

        @pl.when((s <= 3) & (z <= NZ - 2))
        def _():
            to(slot + 2, kv_send_z.at[s, h], above)

        @pl.when(xh == 0)
        def _():
            to(slot + 1, kv_send_x.at[s, h], partner)

        @pl.when((xh == 1) & (s >= 1))
        def _():
            to(slot - 1, kv_send_x.at[s, h], partner)

        @pl.when((xh == 1) & (s == 4) & (z <= NZ - 2))
        def _():
            to(9, kv_send_9.at[h], (d, c + 1, t))

    forward_kv(0, 0)
    forward_kv(0, 1)

    x_pair = (d + 1 - 2 * xl, c, t)
    x_other = (d + 1 - 2 * xl, c + 1 - 2 * xh, t)
    owners = [owner_ref[m] for m in range(4)]
    bx_copies = []
    for half, device in enumerate((x_pair, x_other)):
        for n, (source, rows) in enumerate(zip(mine_of(half), (pl.ds(0, 256), pl.ds(256, 32)))):
            bx_copies.append(
                remote(source, bx.at[half, xl, rows], bx_send.at[half, n], bx_recv.at[half, n], device)
            )
    for copy in bx_copies:
        copy.start()

    def columns_of(p):
        p = p + odd_z * (1 - 2 * lax.rem(p, 2))
        return pl.ds(pl.multiple_of(p * 512, 512), 512)

    def send_inputs(steps):
        for core, source in enumerate((x_ref, gl_ref)):
            @pl.when(t == core)
            def _():
                for k in steps:
                    other, device = plane_device(k)
                    remote(
                        source.at[0, :, columns_of(other)], xr.at[core, plane], a_send.at[k], a_recv.at[plane], device
                    ).start()
                if 4 in steps:
                    local(source.at[0, :, columns_of(plane)], xr.at[core, plane], load_sem.at[7]).start()

    send_inputs((4, 8, 12))

    def y_device(k):
        return (lax.rem(y + k, NY) * NX + xl, c, t)

    by_copies = [
        remote(pk.at[odd if k == 2 else 1 - odd], by.at[y], by_send.at[k], by_recv.at[y], y_device(k))
        for k in range(1, NY)
    ]

    def pick_x():
        for copy in b_loads:
            copy.wait()
        for copy in bx_copies:
            copy.wait_recv()
        for half, (wide, narrow) in enumerate(((0, 1), (3, 2))):
            pk[half, 0:256] = bx[half, lax.rem(owners[wide], NX), 0:256]
            pk[half, 256:288] = bx[half, lax.rem(owners[narrow], NX), 256:288]
        for copy in by_copies:
            copy.start()

    def pick_y():
        by[y] = pk[odd]
        for k in range(1, NY):
            yy = lax.rem(y + k, NY)
            arrived(by.at[yy], by_recv.at[yy])
        wide = jnp.where(odd == 0, owners[0], owners[3])
        narrow = jnp.where(odd == 0, owners[1], owners[2])
        bas[odd, z, 0:256] = by[lax.div(wide, NX), 0:256]
        bas[odd, z, 256:288] = by[lax.div(narrow, NX), 256:288]

    z_up = (d, lax.rem(z + 1, NZ) * NX + xh, t)
    z_down = (d, lax.rem(z + NZ - 1, NZ) * NX + xh, t)
    LOW, HIGH = pl.ds(0, 144), pl.ds(144, 144)

    def part_of(p):
        return lax.rem(p + 2 * NZ, NZ)

    def ring_parts(k, ways):
        parts = []
        for way, device, p in ways:
            ref = bas.at[odd, part_of(p)]
            if k == 3:
                ref = ref.at[(LOW, HIGH)[way]]
            parts.append((ref, ring_send.at[way, k], ring_recv.at[way, k], device))
        return parts

    def ring_copies(k):
        parts = ring_parts(k, ((0, z_up, z - k), (1, z_down, z + k)))
        return [remote(ref, ref, send, recv, device) for ref, send, recv, device in parts]

    def y_forward(p):
        p = part_of(p)
        return [
            remote(ref, ref, yf_send.at[n, p], yf_recv.at[n, p], y_device(k))
            for n, (ref, k) in enumerate(((bas.at[odd, p, LOW], 1), (bas.at[odd, p, HIGH], 3)))
        ]

    def ring_step(k):
        if k >= 1:
            for ref, _, recv, _ in ring_parts(k - 1, ((0, z_up, z - k), (1, z_down, z + k))):
                arrived(ref, recv)
        if k <= 3:
            for copy in ring_copies(k):
                copy.start()
        for p in ((z - k, z + k) if 1 <= k <= 3 else (z + k,)):
            for copy in y_forward(p):
                copy.start()

    def odd_slot(j):
        arrived(kvg.at[j, 0], kv_recv.at[j, 0])
        score(j)

    def forward_step(s):
        @pl.when(z >= s)
        def _():
            arrived(kvg.at[2 * s, 0], kv_recv.at[2 * s, 0])
            forward_kv(s, 0)
            score(2 * s)
            arrived(kvg.at[2 * s, 1], kv_recv.at[2 * s, 1])
            forward_kv(s, 1)

        @pl.when((s >= 2) & (z + xh >= s - 1))
        def _():
            odd_slot(2 * s - 3)

        @pl.when(s == 2)
        def _():
            pick_x()

    loop(1, 5, forward_step)
    pick_y()
    ring_step(0)

    def last_slots(s):
        @pl.when(z + xh >= s)
        def _():
            odd_slot(2 * s - 1)

    loop(4, 6, last_slots)

    def odd_values(s):
        @pl.when(z + xh >= s)
        def _():
            arrived(kvg.at[2 * s - 1, 1], kv_recv.at[2 * s - 1, 1])

    loop(1, 6, odd_values)
    ring_step(1)

    send_inputs((1, 2, 3, 5, 6, 7))

    den[...] = jnp.zeros_like(den)
    ot[...] = jnp.zeros_like(ot)
    dqt[...] = jnp.zeros_like(dqt)

    def weigh(j):
        for g in range(2):
            value = kvg[j, 1, :, g * HEAD:(g + 1) * HEAD]
            p = jnp.exp(w[j, g] - mx[g])
            w[j, g] = p
            den[g] += jnp.sum(p, axis=0, keepdims=True)
            ot[g] += dot(value, p.astype(BF16), ((0,), (0,)))

    loop(0, jnp.minimum(c, LONGEST - 1) + 1, weigh)
    for g in range(2):
        den[g] = 1.0 / den[g]

    def finish_heads(h):
        g, i = lax.div(h, 8), lax.rem(h, 8)
        columns = pl.ds(pl.multiple_of(h * HEAD, HEAD), HEAD)
        rows = pl.ds(pl.multiple_of(i * HEAD, HEAD), HEAD)
        low = (ot[g, :, rows] * den[g, :, rows]).astype(BF16)
        wide = low.astype(F32) * dot_[g, :, rows].astype(F32)
        delta[g, :, rows] = jnp.sum(wide, axis=0, keepdims=True)
        att_out[0, :, columns] = low.T

    loop(0, 16, finish_heads)
    ring_step(2)

    def backward(j, store):
        for g in range(2):
            columns = slice(g * HEAD, (g + 1) * HEAD)
            key = kvg[j, 0, :, columns]
            value = kvg[j, 1, :, columns]
            p = w[j, g] * den[g]
            ds = (p * (dot(value, dot_[g]) - delta[g])).astype(BF16)
            dqt[g] += dot(key, ds, ((0,), (0,)))
            store(0, columns, dot(ds, qs[g]) * INV_ROOT)
            store(1, columns, dot(p.astype(BF16), dos[g]))

    def chain(s):
        @pl.when(z >= s)
        def _():
            @pl.when((xh == 0) | (s >= 1))
            def _():
                arrived(xrecv.at[s], x_recv.at[s])
                dacc[s] += xrecv[s].astype(F32)

            @pl.when((s == 4) & (xh == 1) & (z <= NZ - 2))
            def _():
                arrived(ext, ext_recv.at[0])
                dacc[s] += ext[...].astype(F32)

            for h in range(2):
                @pl.when((s <= 3) & (z <= NZ - 2))
                def _():
                    arrived(tin.at[s, h], t_recv.at[s, h])
                    dacc[s, h] += tin[s, h].astype(F32)

                @pl.when(s >= 1)
                def _():
                    dsend[2 * s, h] = dacc[s, h].astype(BF16)
                    remote(
                        dsend.at[2 * s, h], tin.at[s - 1, h], t_send.at[s, h], t_recv.at[s - 1, h], below
                    ).start()

    def backward_step(i):
        s = 4 - i

        @pl.when(z + xh >= s + 1)
        def _():
            def store(which, columns, val):
                dsend[2 * s + 1, which, :, columns] = val.astype(BF16)

            backward(2 * s + 1, store)

            @pl.when(xh == 1)
            def _():
                remote(dsend.at[2 * s + 1], xrecv.at[s], x_send.at[s], x_recv.at[s], partner).start()

            @pl.when((xh == 0) & (s <= 3))
            def _():
                remote(dsend.at[2 * s + 1], xrecv.at[s + 1], x_send.at[s], x_recv.at[s + 1], partner).start()

            @pl.when((xh == 0) & (s == 4))
            def _():
                remote(dsend.at[9], ext, ext_send.at[0], ext_recv.at[0], (d, c - 1, t)).start()

        @pl.when(z >= s)
        def _():
            def store(which, columns, val):
                dacc[s, which, :, columns] = val

            backward(2 * s, store)

        @pl.when(i >= 3)
        def _():
            chain(s + 3)

        @pl.when(i == 1)
        def _():
            ring_step(3)

        @pl.when(i == 3)
        def _():
            ring_step(4)

    loop(0, 5, backward_step)
    chain(2)
    send_inputs((9, 10, 11, 13, 14, 15))

    def finish_grads(h):
        g, i = lax.div(h, 8), lax.rem(h, 8)
        columns = pl.ds(pl.multiple_of(h * HEAD, HEAD), HEAD)
        rows = pl.ds(pl.multiple_of(i * HEAD, HEAD), HEAD)
        gq_out[0, :, columns] = (dqt[g, :, rows] * INV_ROOT).astype(BF16).T

    loop(0, 16, finish_grads)
    chain(1)

    for n in range(2):
        for p in range(NZ):
            arrived(bas.at[1 - odd, p, (LOW, HIGH)[n]], yf_recv.at[n, p])

    low_half = pl.ds(pl.multiple_of(t * 128, 128), 128)
    high_half = pl.ds(pl.multiple_of((1 - t) * 128, 128), 128)

    def give(part, pairs):
        for n, (rows, basis) in enumerate(pairs):
            pm[part, n] = dot(rows, basis)
            sx[part, n] = pm[part, n, :, high_half].astype(BF16)
        copy = remote(sx.at[part], rx.at[part], sib_send.at[1 + part], sib_recv.at[1 + part], sibling)
        copy.start()
        return copy

    quad = xl * NX + xh

    def m_parts(part, n, stage, k):
        if n == stage:
            other = lax.rem(quad + k, 4)
            device = (y * NX + lax.div(other, NX), z * NX + lax.rem(other, NX), t)
            mine, theirs = quad, other
        else:
            other = lax.rem(y + k, NY)
            device = (other * NX + xl, c, t)
            mine, theirs = y, other
        lanes = pl.ds(n * 128, 128)

        def ref(at):
            if stage == 0:
                return mm.at[part, y, at, :, lanes] if n == 0 else mm.at[part, at, quad, :, lanes]
            return mm.at[part, at, :, :, lanes] if n == 0 else mm.at[part, :, at, :, lanes]

        return (
            lambda: remote(
                ref(mine), ref(mine), m_send.at[part, n, stage, k], m_recv.at[part, n, stage, mine], device
            ),
            (ref(theirs), m_recv.at[part, n, stage, theirs]),
        )

    def m_start(part, stage):
        for n in range(2):
            loop(1, 4, lambda k: m_parts(part, n, stage, k)[0]().start())

    def m_arrived(part, stage):
        for n in range(2):
            loop(1, 4, lambda k: arrived(*m_parts(part, n, stage, k)[1]))

    def spread(part):
        arrived(rx.at[part], sib_recv.at[1 + part])
        for n in range(2):
            share = pm[part, n, :, low_half] + rx[part, n].astype(F32)
            mm[part, y, quad, :, n * 128:(n + 1) * 128] = share.astype(BF16)
        m_start(part, 0)

    def wide_basis(half):
        return bas[half, :, 0:256, :].reshape(NZ * 256, 256)

    def narrow_basis(half):
        return bas[half, :, 256:288, :].reshape(NZ * 32, 256)

    give_a = give(0, ((att_out[0], wide_basis(1)), (gq_out[0], wide_basis(0))))
    spread(0)
    chain(0)
    for h in range(2):
        gkv_out[h, 0] = dacc[0, h].astype(BF16)
    give_b = give(1, ((gkv_out[0, 0], narrow_basis(0)), (gkv_out[1, 0], narrow_basis(1))))
    spread(1)
    m_arrived(0, 0)
    m_start(0, 1)
    for m, value in enumerate((wide_basis(0), narrow_basis(0), narrow_basis(1), wide_basis(1))):
        wide = value.astype(F32)
        ssq[m:m + 1, :] = jnp.sum(wide * wide, axis=0, keepdims=True)
    give_s = remote(ssq, rssq, sib_send.at[3], sib_recv.at[3], sibling)
    give_s.start()


    local(xr.at[t, plane], xr.at[t, plane], load_sem.at[7]).wait()

    def a_arrived(k):
        other = lax.rem(plane + k, PLANE)
        arrived(xr.at[t, other], a_recv.at[other])

    loop(1, PLANE, a_arrived)
    hand_over = remote(xr.at[t], xr.at[t], sib_send.at[0], sib_recv.at[0], sibling)
    hand_over.start()

    def turn(a):
        def one(p):
            for n in range(4):
                xt[a, n * 128:(n + 1) * 128, pl.ds(pl.multiple_of(p * 128, 128), 128)] = (
                    xr[a, p, :, n * 128:(n + 1) * 128].T
                )
        loop(0, PLANE, one)

    turn(t)
    m_arrived(1, 0)
    m_start(1, 1)
    arrived(xr.at[1 - t], sib_recv.at[0])
    turn(1 - t)

    def piece_device(k):
        zz = side * 4 + lax.div(k, 2)
        return zz, lax.rem(k, 2)

    def reduce_out(part):
        def one(k):
            zz, xx = piece_device(k)
            own = (zz == z) & (xx == xh)

            @pl.when(own)
            def _():
                rr[part, z] = rs[part, k]

            @pl.when(jnp.logical_not(own))
            def _():
                remote(
                    rs.at[part, k], rr.at[part, z], r_send.at[part, k], r_recv.at[part, z],
                    (d, zz * NX + xx, t),
                ).start()

        loop(0, 8, one)

    def outer(part):
        m_arrived(part, 1)

        def one(n):
            rows = pl.ds(pl.multiple_of(n * 128, 128), 128)
            if part == 0:
                out = dot(xt[1, rows, :], mm[0, :, :, :, 0:128].reshape(PLANE * 128, 128))
                gq = dot(xt[0, rows, :], mm[0, :, :, :, 128:256].reshape(PLANE * 128, 128))
                val = jnp.concatenate([out, gq], axis=1)
            else:
                val = dot(xt[0, rows, :], mm[1].reshape(PLANE * 128, 256))
            rs[part, pl.ds(2 * n, 2)] = val.astype(BF16).reshape(2, 64, 256)

        loop(0, 4, one)
        reduce_out(part)

    outer(0)
    outer(1)

    source = lax.div(z, 4)

    def r_arrived(part):
        def one(zz):
            @pl.when(jnp.logical_not((source == side) & (zz == z)))
            def _():
                arrived(rr.at[part, zz], r_recv.at[part, zz])
        loop(0, NZ, one)

    arrived(rssq, sib_recv.at[3])
    rssq[...] = lax.rsqrt(ssq[...] + rssq[...] + 1e-06) * (1.0 / 128.0)
    for part, places in ((0, (3, 0)), (1, (1, 2))):
        r_arrived(part)
        total = jnp.sum(rr[part].astype(F32), axis=0)
        for n, m in enumerate(places):
            proj_out[:, m, :] = total[:, n * 128:(n + 1) * 128] * rssq[m:m + 1, low_half]

    def kv_left(s):
        for h in range(2):
            @pl.when((z >= s) & (s <= 3) & (z <= NZ - 2))
            def _():
                left(kvg.at[0, h], kv_send_z.at[s, h])

            @pl.when((z >= s) & ((xh == 0) | (s >= 1)))
            def _():
                left(kvg.at[0, h], kv_send_x.at[s, h])

            @pl.when((z >= s) & (s >= 1))
            def _():
                left(dsend.at[0, h], t_send.at[s, h])

        @pl.when((z + xh >= s + 1) & ((xh == 1) | (s <= 3)))
        def _():
            left(dsend.at[0], x_send.at[s])

    loop(0, 5, kv_left)

    @pl.when((xh == 1) & (z >= 4) & (z <= NZ - 2))
    def _():
        for h in range(2):
            left(kvg.at[0, h], kv_send_9.at[h])

    @pl.when((xh == 0) & (z >= 5))
    def _():
        left(dsend.at[0], ext_send.at[0])

    for copy in bx_copies + by_copies:
        copy.wait_send()
    for k in range(4):
        for copy in ring_copies(k):
            copy.wait_send()
    for n in range(2):
        for p in range(NZ):
            left(bas.at[0, 0, LOW], yf_send.at[n, p])
    for part in range(2):
        for n in range(2):
            for stage in range(2):
                loop(1, 4, lambda k: m_parts(part, n, stage, k)[0]().wait_send())

    def plane_left(k):
        left(xr.at[0, 0], a_send.at[k])

    loop(1, PLANE, plane_left)
    for copy in (hand_over, give_a, give_b, give_s):
        copy.wait_send()

    def reduce_left(k):
        zz, xx = piece_device(k)

        @pl.when(jnp.logical_not((zz == z) & (xx == xh)))
        def _():
            left(rs.at[0, 0], r_send.at[0, k])
            left(rs.at[1, 0], r_send.at[1, k])

    loop(0, 8, reduce_left)


def on_device(*args):
    dma = pltpu.SemaphoreType.DMA
    vmem = pltpu.VMEM
    scratch = [
        vmem((128, 2048), BF16), vmem((128, 2048), BF16),
        vmem((2, 1024, 128), BF16), vmem((2, 1024, 128), BF16),
        vmem((2, 128, 1024), BF16), vmem((2, 128, 1024), BF16),
        vmem((LONGEST, 2, 128, 256), BF16),
        vmem((LONGEST, 2, 128, 1024), F32),
        vmem((2, 1, 1024), F32), vmem((2, 1, 1024), F32), vmem((2, 1, 1024), F32),
        vmem((2, 128, 1024), F32), vmem((2, 128, 1024), F32),
        vmem((LONGEST, 2, 128, 256), BF16), vmem((5, 2, 128, 256), F32),
        vmem((5, 2, 128, 256), BF16), vmem((4, 2, 128, 256), BF16),
        vmem((2, 128, 256), BF16),
        vmem((2, 2, 288, 256), BF16), vmem((2, 288, 256), BF16), vmem((4, 288, 256), BF16),
        vmem((2, NZ, 288, 256), BF16),
        vmem((2, PLANE, 128, 512), BF16), vmem((2, 512, 2048), BF16),
        vmem((2, 2, 128, 256), F32), vmem((2, 2, 128, 128), BF16), vmem((2, 2, 128, 128), BF16),
        vmem((2, 4, 4, 128, 256), BF16),
        vmem((2, 8, 64, 256), BF16), vmem((2, 8, 64, 256), BF16),
        vmem((4, 256), F32), vmem((4, 256), F32),
        dma((8,)),
        dma((10, 2)), dma((4, 2)), dma((5, 2)), dma((2,)),
        dma((5,)), dma((5,)), dma((5, 2)), dma((4, 2)), dma((1,)), dma((1,)),
        dma((2, 2)), dma((2, 2)), dma((4,)), dma((4,)), dma((2, 4)), dma((2, 4)), dma((2, NZ)), dma((2, NZ)),
        dma((PLANE,)), dma((PLANE,)), dma((4,)), dma((4,)),
        dma((2, 2, 2, 4)), dma((2, 2, 2, 4)), dma((2, 8)), dma((2, 8)),
    ]
    hbm = pl.BlockSpec(memory_space=pl.ANY)
    smem = pl.BlockSpec(memory_space=pltpu.SMEM)
    return pl.pallas_call(
        kernel,
        out_shape=(
            pltpu.VMEM((1, 128, 2048), BF16),
            pltpu.VMEM((1, 128, 2048), BF16),
            pltpu.VMEM((2, 1, 128, 256), BF16),
            pltpu.VMEM((64, 4, 128), F32),
        ),
        in_specs=[hbm] * 5 + [smem] + [hbm] * 2 + [smem],
        out_specs=(pl.BlockSpec(memory_space=pltpu.VMEM),) * 4,
        scratch_shapes=scratch,
        compiler_params=pltpu.CompilerParams(
            collective_id=0, has_side_effects=True, vmem_limit_bytes=60 * 1024 * 1024
        ),
        cost_estimate=pl.CostEstimate(flops=7_000_000_000, bytes_accessed=12_000_000, transcendentals=3_000_000),
    )(*args)


def solution(mesh):
    return jax.shard_map(
        on_device,
        mesh=mesh,
        in_specs=(
            P("dp", "ctx", None),
            P("dp", "ctx", "tp"),
            P(None, "dp", "ctx", "tp"),
            P("dp", "ctx", "tp"),
            P("dp", "ctx", None),
            P("dp", None),
            P(None, "dp", None, None),
            P(None, "dp", None, None),
            P(),
        ),
        out_specs=(
            P("dp", "ctx", "tp"),
            P("dp", "ctx", "tp"),
            P(None, "dp", "ctx", "tp"),
            P(("dp", "ctx"), None, "tp"),
        ),
        check_vma=False,
    )
```

```python
import math

import jax
import jax.numpy as jnp
from jax import lax
from jax.experimental import pallas as pl
from jax.experimental.pallas import tpu as pltpu
from jax.sharding import PartitionSpec as P

HEAD = 128
BLOCK = 128
LONGEST = 10
NEG = -1e30
MESH = pl.DeviceIdType.MESH
BF16 = jnp.bfloat16
F32 = jnp.float32
INV_ROOT = 1.0 / math.sqrt(HEAD)

NX = 2
NY = 4
NZ = 8


def dot(a, b, dims=((1,), (0,))):
    return lax.dot_general(a, b, (dims, ((), ())), preferred_element_type=F32)


def kernel(
    x_ref, q_ref, kv_ref, do_ref, gl_ref, docs_ref, wide_ref, narrow_ref, owner_ref,
    att_out, gq_out, gkv_out, proj_out,
    qf, dof, qs, dos, qt, dot_, kvg, w, mx, at, den, delta, ot, otl, dqt,
    dsend, dacc, xrecv, tin, ext,
    bx, pk, by, bas, relay, xr, xt, pm, sx, rx, mm, rs, rr, rs2, rr2, ssq, rssq,
    load_sem,
    kv_recv, kv_send_z, kv_send_x, kv_send_9,
    x_send, x_recv, t_send, t_recv, ext_send, ext_recv,
    bx_send, bx_recv, by_send, by_recv, ring_send, ring_recv, yf_send, yf_recv,
    a_send, a_recv, relay_send, relay_recv, sib_send, sib_recv, m_send, m_recv, r_send, r_recv, z_send, z_recv,
):
    d = lax.axis_index("dp")
    c = lax.axis_index("ctx")
    t = lax.axis_index("tp")
    y, xl = lax.div(d, NX), lax.rem(d, NX)
    z, xh = lax.div(c, NX), lax.rem(c, NX)
    odd = lax.rem(y, 2)
    partner = (d, c + 1 - 2 * xh, t)
    above = (d, c + NX, t)
    below = (d, c - NX, t)
    sibling = (d, c, 1 - t)

    def local(src, dst, sem):
        return pltpu.make_async_copy(src, dst, sem)

    def remote(src, dst, send, recv, device):
        return pltpu.make_async_remote_copy(
            src_ref=src, dst_ref=dst, send_sem=send, recv_sem=recv,
            device_id=device, device_id_type=MESH,
        )

    def arrived(dst, recv):
        remote(dst, dst, recv, recv, sibling).wait_recv()

    def left(src, send):
        remote(src, src, send, send, sibling).wait_send()

    def loop(low, high, body):
        def step(i, carry):
            body(i)
            return carry
        lax.fori_loop(low, high, step, 0)

    q_load = local(q_ref.at[0], qf, load_sem.at[0])
    do_load = local(do_ref.at[0], dof, load_sem.at[1])
    kv_load = local(kv_ref.at[:, 0], kvg.at[0], load_sem.at[2])

    def mine_of(half):
        return (
            wide_ref.at[half, 0, pl.ds(pl.multiple_of(t * 2048 + z * 256, 256), 256), :],
            narrow_ref.at[half, 0, pl.ds(pl.multiple_of(t * 256 + z * 32, 32), 32), :],
        )

    b_loads = []
    for half in range(2):
        for n, (source, rows) in enumerate(zip(mine_of(half), (pl.ds(0, 256), pl.ds(256, 32)))):
            b_loads.append(local(source, bx.at[half, xl, rows], load_sem.at[3 + 2 * half + n]))
    barrier = pltpu.get_barrier_semaphore()

    def greet(device):
        pl.semaphore_signal(barrier, inc=1, device_id=device, device_id_type=MESH)

    def y_device(k):
        return (lax.rem(y + k, NY) * NX + xl, c, t)

    def dp_device(k):
        other = lax.rem(d + k, NX * NY)
        return other, (other, c, t)

    loop(1, NX * NY, lambda k: greet(dp_device(k)[1]))
    greet(partner)
    greet((d + 1 - 2 * xl, c + 1 - 2 * xh, t))

    place = xl * NY + y

    def greet_column(k):
        zz = lax.rem(z + k, NZ)
        greet((d, zz * NX, t))
        greet((d, zz * NX + 1, t))

    loop(1, NZ, greet_column)
    greet(sibling)
    kv_load.start()
    q_load.start()
    do_load.start()
    for copy in b_loads:
        copy.start()

    def attend(j, diagonal=False):
        if not diagonal:
            same = docs_ref[0, c] == docs_ref[0, c - j]
            bias = jnp.where(same, 0.0, NEG).astype(F32)
        for g in range(2):
            columns = slice(g * HEAD, (g + 1) * HEAD)
            s = dot(kvg[j, 0, :, columns], qt[g]) * INV_ROOT
            if diagonal:
                rows = lax.broadcasted_iota(jnp.int32, s.shape, 0)
                lanes = lax.broadcasted_iota(jnp.int32, s.shape, 1) & (BLOCK - 1)
                s = jnp.where(rows <= lanes, s, NEG)
                top = jnp.max(s, axis=0, keepdims=True)
            else:
                s = s + bias
                top = jnp.maximum(mx[g], jnp.max(s, axis=0, keepdims=True))
            p = jnp.exp(s - top)
            w[j, g] = p
            at[j, g] = top
            term = dot(kvg[j, 1, :, columns], p.astype(BF16), ((0,), (0,)))
            total = jnp.sum(p, axis=0, keepdims=True)
            if not diagonal:
                factor = jnp.exp(mx[g] - top)
                term += ot[g] * factor
                total += den[g] * factor
            mx[g] = top
            ot[g] = term
            den[g] = total

    pl.semaphore_wait(barrier, (NX * NY - 1) + 2 + 2 * (NZ - 1) + 1)

    def forward_kv(s, h):
        slot = 2 * s

        def to(dst, send, device):
            remote(kvg.at[slot, h], kvg.at[dst, h], send, kv_recv.at[dst, h], device).start()

        @pl.when((s <= 3) & (z <= NZ - 2))
        def _():
            to(slot + 2, kv_send_z.at[s, h], above)

        @pl.when(xh == 0)
        def _():
            to(slot + 1, kv_send_x.at[s, h], partner)

        @pl.when((xh == 1) & (s >= 1))
        def _():
            to(slot - 1, kv_send_x.at[s, h], partner)

        @pl.when((xh == 1) & (s == 4) & (z <= NZ - 2))
        def _():
            to(9, kv_send_9.at[h], (d, c + 1, t))

    kv_load.wait()
    forward_kv(0, 0)
    forward_kv(0, 1)

    x_pair = (d + 1 - 2 * xl, c, t)
    x_other = (d + 1 - 2 * xl, c + 1 - 2 * xh, t)
    owners = [owner_ref[m] for m in range(4)]
    bx_copies = []
    for half, device in enumerate((x_pair, x_other)):
        for n, (source, rows) in enumerate(zip(mine_of(half), (pl.ds(0, 256), pl.ds(256, 32)))):
            bx_copies.append(
                remote(source, bx.at[half, xl, rows], bx_send.at[half, n], bx_recv.at[half, n], device)
            )
    for copy in bx_copies:
        copy.start()

    def send_inputs(steps):
        for core, source in enumerate((x_ref, gl_ref)):
            @pl.when(t == core)
            def _():
                for dy, dx in steps:
                    row = lax.rem(y + dy, NY)
                    other = row * NX + side(dx)
                    part = source.at[0, :, pl.ds(pl.multiple_of(other * 1024, 1024), 1024)]
                    send = a_send.at[dy * NX + dx]
                    if dy == dx == 0:
                        local(part, xr.at[core, place], load_sem.at[7]).start()
                    elif dy == 0:
                        remote(part, xr.at[core, place], send, a_recv.at[place], x_pair).start()
                    elif dx == 0:
                        remote(part, xr.at[core, place], send, a_recv.at[place], y_device(dy)).start()
                    else:
                        remote(part, relay.at[y], send, relay_recv.at[y], y_device(dy)).start()

    def relay_copy(k):
        row = lax.rem(y + k, NY)
        slot = xl * NY + row
        return remote(relay.at[row], xr.at[t, slot], relay_send.at[row], a_recv.at[slot], x_pair)

    def relay_on(k):
        row = lax.rem(y + k, NY)
        arrived(relay.at[row], relay_recv.at[row])
        relay_copy(k).start()

    def side(dx):
        return xl if dx == 0 else 1 - xl

    send_inputs(((1, 0), (3, 0), (0, 0), (1, 1), (3, 1)))

    def split_heads(h):
        g, i = lax.div(h, 8), lax.rem(h, 8)
        columns = pl.ds(pl.multiple_of(h * HEAD, HEAD), HEAD)
        rows = pl.ds(pl.multiple_of(i * HEAD, HEAD), HEAD)
        tile = qf[:, columns]
        qs[g, rows, :] = tile
        qt[g, :, rows] = tile.T
        tile = dof[:, columns]
        dos[g, rows, :] = tile
        dot_[g, :, rows] = tile.T

    q_load.wait()
    do_load.wait()
    loop(0, 16, split_heads)
    attend(0, True)

    by_copies = [
        remote(pk.at[odd if k == 2 else 1 - odd], by.at[y], by_send.at[k], by_recv.at[y], y_device(k))
        for k in range(1, NY)
    ]

    def pick_x():
        for copy in b_loads:
            copy.wait()
        for copy in bx_copies:
            copy.wait_recv()
        for half, (wide, narrow) in enumerate(((0, 1), (3, 2))):
            pk[half, 0:256] = bx[half, lax.rem(owners[wide], NX), 0:256]
            pk[half, 256:288] = bx[half, lax.rem(owners[narrow], NX), 256:288]
        for copy in by_copies:
            copy.start()

    def pick_y():
        by[y] = pk[odd]
        for k in range(1, NY):
            yy = lax.rem(y + k, NY)
            arrived(by.at[yy], by_recv.at[yy])
        wide = jnp.where(odd == 0, owners[0], owners[3])
        narrow = jnp.where(odd == 0, owners[1], owners[2])
        bas[odd, z, 0:256] = by[lax.div(wide, NX), 0:256]
        bas[odd, z, 256:288] = by[lax.div(narrow, NX), 256:288]

    z_up = (d, lax.rem(z + 1, NZ) * NX + xh, t)
    z_down = (d, lax.rem(z + NZ - 1, NZ) * NX + xh, t)
    LOW, HIGH = pl.ds(0, 144), pl.ds(144, 144)

    def part_of(p):
        return lax.rem(p + 2 * NZ, NZ)

    def ring_parts(k, ways):
        parts = []
        for way, device, p in ways:
            ref = bas.at[odd, part_of(p)]
            if k == 3:
                ref = ref.at[(LOW, HIGH)[way]]
            parts.append((ref, ring_send.at[way, k], ring_recv.at[way, k], device))
        return parts

    def ring_copies(k):
        parts = ring_parts(k, ((0, z_up, z - k), (1, z_down, z + k)))
        return [remote(ref, ref, send, recv, device) for ref, send, recv, device in parts]

    def y_forward(p):
        p = part_of(p)
        return [
            remote(ref, ref, yf_send.at[n, p], yf_recv.at[n, p], y_device(k))
            for n, (ref, k) in enumerate(((bas.at[odd, p, LOW], 1), (bas.at[odd, p, HIGH], 3)))
        ]

    def ring_step(k):
        if k >= 1:
            for ref, _, recv, _ in ring_parts(k - 1, ((0, z_up, z - k), (1, z_down, z + k))):
                arrived(ref, recv)
        if k <= 3:
            for copy in ring_copies(k):
                copy.start()
        for p in ((z - k, z + k) if 1 <= k <= 3 else (z + k,)):
            for copy in y_forward(p):
                copy.start()

    def odd_slot(j):
        arrived(kvg.at[j, 0], kv_recv.at[j, 0])
        arrived(kvg.at[j, 1], kv_recv.at[j, 1])
        attend(j)

    def forward_step(s):
        @pl.when(z >= s)
        def _():
            arrived(kvg.at[2 * s, 0], kv_recv.at[2 * s, 0])
            forward_kv(s, 0)
            arrived(kvg.at[2 * s, 1], kv_recv.at[2 * s, 1])
            forward_kv(s, 1)
            attend(2 * s)

        @pl.when((s >= 2) & (z + xh >= s - 1))
        def _():
            odd_slot(2 * s - 3)

        @pl.when(s == 2)
        def _():
            pick_x()

    loop(1, 5, forward_step)
    pick_y()
    ring_step(0)

    def last_slots(s):
        @pl.when(z + xh >= s)
        def _():
            odd_slot(2 * s - 1)

    loop(4, 6, last_slots)

    send_inputs(((0, 1), (2, 0), (2, 1)))

    dqt[...] = jnp.zeros_like(dqt)
    for g in range(2):
        den[g] = 1.0 / den[g]
        low = (ot[g] * den[g]).astype(BF16)
        otl[g] = low
        delta[g] = jnp.sum(low.astype(F32) * dot_[g].astype(F32), axis=0, keepdims=True)

    def scale(j):
        for g in range(2):
            at[j, g] = jnp.exp(at[j, g] - mx[g]) * den[g]

    loop(0, jnp.minimum(c, LONGEST - 1) + 1, scale)
    ring_step(1)

    def backward(j, store):
        for g in range(2):
            columns = slice(g * HEAD, (g + 1) * HEAD)
            key = kvg[j, 0, :, columns]
            value = kvg[j, 1, :, columns]
            p = w[j, g] * at[j, g]
            ds = (p * (dot(value, dot_[g]) - delta[g])).astype(BF16)
            dqt[g] += dot(key, ds, ((0,), (0,)))
            store(0, columns, dot(ds, qs[g]) * INV_ROOT)
            store(1, columns, dot(p.astype(BF16), dos[g]))

    def chain(s):
        @pl.when(z >= s)
        def _():
            @pl.when((xh == 0) | (s >= 1))
            def _():
                arrived(xrecv.at[s], x_recv.at[s])
                dacc[s] += xrecv[s].astype(F32)

            @pl.when((s == 4) & (xh == 1) & (z <= NZ - 2))
            def _():
                arrived(ext, ext_recv.at[0])
                dacc[s] += ext[...].astype(F32)

            for h in range(2):
                @pl.when((s <= 3) & (z <= NZ - 2))
                def _():
                    arrived(tin.at[s, h], t_recv.at[s, h])
                    dacc[s, h] += tin[s, h].astype(F32)

                @pl.when(s >= 1)
                def _():
                    dsend[2 * s, h] = dacc[s, h].astype(BF16)
                    remote(
                        dsend.at[2 * s, h], tin.at[s - 1, h], t_send.at[s, h], t_recv.at[s - 1, h], below
                    ).start()

    def backward_step(i):
        s = 4 - i

        @pl.when(z + xh >= s + 1)
        def _():
            def store(which, columns, val):
                dsend[2 * s + 1, which, :, columns] = val.astype(BF16)

            backward(2 * s + 1, store)

            @pl.when(xh == 1)
            def _():
                remote(dsend.at[2 * s + 1], xrecv.at[s], x_send.at[s], x_recv.at[s], partner).start()

            @pl.when((xh == 0) & (s <= 3))
            def _():
                remote(dsend.at[2 * s + 1], xrecv.at[s + 1], x_send.at[s], x_recv.at[s + 1], partner).start()

            @pl.when((xh == 0) & (s == 4))
            def _():
                remote(dsend.at[9], ext, ext_send.at[0], ext_recv.at[0], (d, c - 1, t)).start()

        @pl.when(z >= s)
        def _():
            def store(which, columns, val):
                dacc[s, which, :, columns] = val

            backward(2 * s, store)

        @pl.when(i == 1)
        def _():
            ring_step(2)

        @pl.when(i == 2)
        def _():
            relay_on(1)

        @pl.when(i == 3)
        def _():
            ring_step(3)

    loop(0, 5, backward_step)
    relay_on(3)
    ring_step(4)
    chain(4)
    relay_on(2)

    def finish_grads(h):
        g, i = lax.div(h, 8), lax.rem(h, 8)
        columns = pl.ds(pl.multiple_of(h * HEAD, HEAD), HEAD)
        rows = pl.ds(pl.multiple_of(i * HEAD, HEAD), HEAD)
        gq_out[0, :, columns] = (dqt[g, :, rows] * INV_ROOT).astype(BF16).T
        att_out[0, :, columns] = otl[g, :, rows].T

    loop(0, 16, finish_grads)
    chain(3)
    hand_overs = [
        remote(ref, ref, sib_send.at[n], sib_recv.at[n], sibling)
        for n, ref in ((0, xr.at[t, pl.ds(xl * NY, NY)]), (4, xr.at[t, pl.ds((1 - xl) * NY, NY)]))
    ]

    def inputs_arrived(dx):
        for k in range(NY):
            at_y = side(dx) * NY + lax.rem(y + k, NY)
            if dx == 0 and k == 0:
                local(xr.at[t, place], xr.at[t, place], load_sem.at[7]).wait()
            else:
                arrived(xr.at[t, at_y], a_recv.at[at_y])
        hand_overs[dx].start()

    def other_arrived(dx):
        arrived(xr.at[1 - t, pl.ds(side(dx) * NY, NY)], sib_recv.at[4 * dx])

    def turn(a, dx):
        def one(n):
            other, group = side(dx) * NY + lax.div(n, 2), lax.rem(n, 2)
            tokens = pl.ds(pl.multiple_of(other * 128, 128), 128)
            for m in range(4):
                rows = pl.ds(pl.multiple_of(group * 512 + m * 128, 128), 128)
                xt[a, rows, tokens] = xr[a, other, :, rows].T
        loop(0, NY * 2, one)

    inputs_arrived(0)
    chain(2)
    turn(t, 0)

    for n in range(2):
        for p in range(NZ):
            arrived(bas.at[1 - odd, p, (LOW, HIGH)[n]], yf_recv.at[n, p])

    low_half = pl.ds(pl.multiple_of(t * 128, 128), 128)
    high_half = pl.ds(pl.multiple_of((1 - t) * 128, 128), 128)

    def give(part, pairs):
        for n, (rows, basis) in enumerate(pairs):
            pm[part, n] = dot(rows, basis)
            sx[part, n] = pm[part, n, :, high_half].astype(BF16)
        copy = remote(sx.at[part], rx.at[part], sib_send.at[1 + part], sib_recv.at[1 + part], sibling)
        copy.start()
        return copy

    def m_copy(part, k):
        ref = mm.at[part, place]
        return remote(ref, ref, m_send.at[part, k], m_recv.at[part, place], dp_device(k)[1])

    def m_arrived(part):
        def one(k):
            other, _ = dp_device(k)
            slot = lax.rem(other, NX) * NY + lax.div(other, NX)
            arrived(mm.at[part, slot], m_recv.at[part, slot])

        loop(1, NX * NY, one)

    def spread(part):
        arrived(rx.at[part], sib_recv.at[1 + part])
        for n in range(2):
            share = pm[part, n, :, low_half] + rx[part, n].astype(F32)
            mm[part, place, :, n * 128:(n + 1) * 128] = share.astype(BF16)
        loop(1, NX * NY, lambda k: m_copy(part, k).start())

    def wide_basis(half):
        return bas[half, :, 0:256, :].reshape(NZ * 256, 256)

    def narrow_basis(half):
        return bas[half, :, 256:288, :].reshape(NZ * 32, 256)

    give_a = give(0, ((att_out[0], wide_basis(1)), (gq_out[0], wide_basis(0))))
    chain(1)
    spread(0)
    other_arrived(0)
    turn(1 - t, 0)

    chain(0)
    for h in range(2):
        gkv_out[h, 0] = dacc[0, h].astype(BF16)
    give_b = give(1, ((gkv_out[0, 0], narrow_basis(0)), (gkv_out[1, 0], narrow_basis(1))))
    spread(1)

    def x_copy(part):
        return remote(rs.at[part, 1 - xh], rr.at[part], r_send.at[part], r_recv.at[part], partner)

    def outer(part):
        tokens = NX * NY * 128

        def one(n):
            rows = pl.ds(pl.multiple_of(n * 256, 256), 256)
            if part == 0:
                out = dot(xt[1, rows, :], mm[0, :, :, 0:128].reshape(tokens, 128))
                gq = dot(xt[0, rows, :], mm[0, :, :, 128:256].reshape(tokens, 128))
                val = jnp.concatenate([out, gq], axis=1).astype(BF16)
            else:
                val = dot(xt[0, rows, :], mm[1].reshape(tokens, 256)).astype(BF16)
            for m in range(2):
                rs[part, 0, 2 * n + m] = val[m * 128:m * 128 + 64]
                rs[part, 1, 2 * n + m] = val[m * 128 + 64:m * 128 + 128]

        loop(0, NZ // 2, one)
        x_copy(part).start()

    def z_copy(part, k):
        zz = lax.rem(z + k, NZ)
        return remote(
            rs2.at[part, zz], rr2.at[part, z], z_send.at[part, k], z_recv.at[part, z], (d, zz * NX + xh, t)
        )

    def over_x(part):
        arrived(rr.at[part], r_recv.at[part])

        def one(zz):
            total = rs[part, xh, zz].astype(F32) + rr[part, zz].astype(F32)
            rs2[part, zz] = total.astype(BF16)

        loop(0, NZ, one)
        loop(1, NZ, lambda k: z_copy(part, k).start())

    def over_z(part, places):
        def one(k):
            zz = lax.rem(z + k, NZ)
            arrived(rr2.at[part, zz], z_recv.at[part, zz])

        loop(1, NZ, one)
        total = rs2[part, z].astype(F32)
        for k in range(1, NZ):
            total += rr2[part, lax.rem(z + k, NZ)].astype(F32)
        for n, m in enumerate(places):
            proj_out[:, m, :] = total[:, n * 128:(n + 1) * 128] * rssq[m:m + 1, low_half]

    inputs_arrived(1)
    turn(t, 1)
    other_arrived(1)
    turn(1 - t, 1)
    m_arrived(0)
    outer(0)
    m_arrived(1)
    outer(1)
    for m, value in enumerate((wide_basis(0), narrow_basis(0), narrow_basis(1), wide_basis(1))):
        wide = value.astype(F32)
        ssq[m:m + 1, :] = jnp.sum(wide * wide, axis=0, keepdims=True)
    give_s = remote(ssq, rssq, sib_send.at[3], sib_recv.at[3], sibling)
    give_s.start()


    over_x(0)
    arrived(rssq, sib_recv.at[3])
    rssq[...] = lax.rsqrt(ssq[...] + rssq[...] + 1e-06) * (1.0 / 128.0)
    over_x(1)
    over_z(0, (3, 0))
    over_z(1, (1, 2))

    def kv_left(s):
        for h in range(2):
            @pl.when((z >= s) & (s <= 3) & (z <= NZ - 2))
            def _():
                left(kvg.at[0, h], kv_send_z.at[s, h])

            @pl.when((z >= s) & ((xh == 0) | (s >= 1)))
            def _():
                left(kvg.at[0, h], kv_send_x.at[s, h])

            @pl.when((z >= s) & (s >= 1))
            def _():
                left(dsend.at[0, h], t_send.at[s, h])

        @pl.when((z + xh >= s + 1) & ((xh == 1) | (s <= 3)))
        def _():
            left(dsend.at[0], x_send.at[s])

    loop(0, 5, kv_left)

    @pl.when((xh == 1) & (z >= 4) & (z <= NZ - 2))
    def _():
        for h in range(2):
            left(kvg.at[0, h], kv_send_9.at[h])

    @pl.when((xh == 0) & (z >= 5))
    def _():
        left(dsend.at[0], ext_send.at[0])

    for copy in bx_copies + by_copies:
        copy.wait_send()
    for k in range(4):
        for copy in ring_copies(k):
            copy.wait_send()
    for n in range(2):
        for p in range(NZ):
            left(bas.at[0, 0, LOW], yf_send.at[n, p])
    def dp_left(k):
        left(xr.at[0, 0], a_send.at[k])
        for part in range(2):
            m_copy(part, k).wait_send()

    loop(1, NX * NY, dp_left)
    for part in range(2):
        x_copy(part).wait_send()
    for k in range(1, NY):
        relay_copy(k).wait_send()
    for part in range(2):
        loop(1, NZ, lambda k: z_copy(part, k).wait_send())
    for copy in (*hand_overs, give_a, give_b, give_s):
        copy.wait_send()


def on_device(*args):
    dma = pltpu.SemaphoreType.DMA
    vmem = pltpu.VMEM
    scratch = [
        vmem((128, 2048), BF16), vmem((128, 2048), BF16),
        vmem((2, 1024, 128), BF16), vmem((2, 1024, 128), BF16),
        vmem((2, 128, 1024), BF16), vmem((2, 128, 1024), BF16),
        vmem((LONGEST, 2, 128, 256), BF16),
        vmem((LONGEST, 2, 128, 1024), F32),
        vmem((2, 1, 1024), F32), vmem((LONGEST, 2, 1, 1024), F32), vmem((2, 1, 1024), F32), vmem((2, 1, 1024), F32),
        vmem((2, 128, 1024), F32), vmem((2, 128, 1024), BF16), vmem((2, 128, 1024), F32),
        vmem((LONGEST, 2, 128, 256), BF16), vmem((5, 2, 128, 256), F32),
        vmem((5, 2, 128, 256), BF16), vmem((4, 2, 128, 256), BF16),
        vmem((2, 128, 256), BF16),
        vmem((2, 2, 288, 256), BF16), vmem((2, 288, 256), BF16), vmem((4, 288, 256), BF16),
        vmem((2, NZ, 288, 256), BF16),
        vmem((NY, 128, 1024), BF16), vmem((2, NX * NY, 128, 1024), BF16), vmem((2, 1024, NX * NY * 128), BF16),
        vmem((2, 2, 128, 256), F32), vmem((2, 2, 128, 128), BF16), vmem((2, 2, 128, 128), BF16),
        vmem((2, NX * NY, 128, 256), BF16),
        vmem((2, NX, NZ, 64, 256), BF16), vmem((2, NZ, 64, 256), BF16),
        vmem((2, NZ, 64, 256), BF16), vmem((2, NZ, 64, 256), BF16),
        vmem((4, 256), F32), vmem((4, 256), F32),
        dma((8,)),
        dma((10, 2)), dma((4, 2)), dma((5, 2)), dma((2,)),
        dma((5,)), dma((5,)), dma((5, 2)), dma((4, 2)), dma((1,)), dma((1,)),
        dma((2, 2)), dma((2, 2)), dma((4,)), dma((4,)), dma((2, 4)), dma((2, 4)), dma((2, NZ)), dma((2, NZ)),
        dma((NX * NY,)), dma((NX * NY,)), dma((NY,)), dma((NY,)), dma((5,)), dma((5,)),
        dma((2, NX * NY)), dma((2, NX * NY)), dma((2,)), dma((2,)), dma((2, NZ)), dma((2, NZ)),
    ]
    hbm = pl.BlockSpec(memory_space=pl.ANY)
    smem = pl.BlockSpec(memory_space=pltpu.SMEM)
    return pl.pallas_call(
        kernel,
        out_shape=(
            pltpu.VMEM((1, 128, 2048), BF16),
            pltpu.VMEM((1, 128, 2048), BF16),
            pltpu.VMEM((2, 1, 128, 256), BF16),
            pltpu.VMEM((64, 4, 128), F32),
        ),
        in_specs=[hbm] * 5 + [smem] + [hbm] * 2 + [smem],
        out_specs=(pl.BlockSpec(memory_space=pltpu.VMEM),) * 4,
        scratch_shapes=scratch,
        compiler_params=pltpu.CompilerParams(
            collective_id=0, has_side_effects=True, vmem_limit_bytes=60 * 1024 * 1024
        ),
        cost_estimate=pl.CostEstimate(flops=7_000_000_000, bytes_accessed=12_000_000, transcendentals=3_000_000),
    )(*args)


def solution(mesh):
    return jax.shard_map(
        on_device,
        mesh=mesh,
        in_specs=(
            P("dp", "ctx", None),
            P("dp", "ctx", "tp"),
            P(None, "dp", "ctx", "tp"),
            P("dp", "ctx", "tp"),
            P("dp", "ctx", None),
            P("dp", None),
            P(None, "dp", None, None),
            P(None, "dp", None, None),
            P(),
        ),
        out_specs=(
            P("dp", "ctx", "tp"),
            P("dp", "ctx", "tp"),
            P(None, "dp", "ctx", "tp"),
            P(("dp", "ctx"), None, "tp"),
        ),
        check_vma=False,
    )
```

```python
import math

import jax
import jax.numpy as jnp
from jax import lax
from jax.experimental import pallas as pl
from jax.experimental.pallas import tpu as pltpu
from jax.sharding import PartitionSpec as P

HEAD = 128
BLOCK = 128
LONGEST = 10
NEG = -1e30
MESH = pl.DeviceIdType.MESH
BF16 = jnp.bfloat16
F32 = jnp.float32
INV_ROOT = 1.0 / math.sqrt(HEAD)

NX = 2
NY = 4
NZ = 8


def dot(a, b, dims=((1,), (0,))):
    return lax.dot_general(a, b, (dims, ((), ())), preferred_element_type=F32)


def kernel(
    x_ref, q_ref, kv_ref, do_ref, gl_ref, docs_ref, wide_ref, narrow_ref, owner_ref,
    att_out, gq_out, gkv_out, proj_out,
    qf, dof, qs, dos, qt, dot_, kvg, w, mx, at, den, delta, ot, otl, dqt,
    dsend, dacc, xrecv, tin, ext,
    bx, pk, by, bas, relay, xr, xt, pm, sx, rx, mm, rs, rr, rs2, rr2, ssq, rssq,
    load_sem,
    kv_recv, kv_send_z, kv_send_x, kv_send_9,
    x_send, x_recv, t_send, t_recv, ext_send, ext_recv,
    bx_send, bx_recv, by_send, by_recv, ring_send, ring_recv, yf_send, yf_recv,
    a_send, a_recv, relay_send, relay_recv, piece_send, piece_recv, sib_send, sib_recv, m_send, m_recv, r_send, r_recv, z_send, z_recv,
):
    d = lax.axis_index("dp")
    c = lax.axis_index("ctx")
    t = lax.axis_index("tp")
    y, xl = lax.div(d, NX), lax.rem(d, NX)
    z, xh = lax.div(c, NX), lax.rem(c, NX)
    odd = lax.rem(y, 2)
    partner = (d, c + 1 - 2 * xh, t)
    above = (d, c + NX, t)
    below = (d, c - NX, t)
    sibling = (d, c, 1 - t)

    def local(src, dst, sem):
        return pltpu.make_async_copy(src, dst, sem)

    def remote(src, dst, send, recv, device):
        return pltpu.make_async_remote_copy(
            src_ref=src, dst_ref=dst, send_sem=send, recv_sem=recv,
            device_id=device, device_id_type=MESH,
        )

    def arrived(dst, recv):
        remote(dst, dst, recv, recv, sibling).wait_recv()

    def left(src, send):
        remote(src, src, send, send, sibling).wait_send()

    def loop(low, high, body):
        def step(i, carry):
            body(i)
            return carry
        lax.fori_loop(low, high, step, 0)

    q_load = local(q_ref.at[0], qf, load_sem.at[0])
    do_load = local(do_ref.at[0], dof, load_sem.at[1])
    kv_load = local(kv_ref.at[:, 0], kvg.at[0], load_sem.at[2])

    def mine_of(half):
        return (
            wide_ref.at[half, 0, pl.ds(pl.multiple_of(t * 2048 + z * 256, 256), 256), :],
            narrow_ref.at[half, 0, pl.ds(pl.multiple_of(t * 256 + z * 32, 32), 32), :],
        )

    b_loads = []
    for half in range(2):
        for n, (source, rows) in enumerate(zip(mine_of(half), (pl.ds(0, 256), pl.ds(256, 32)))):
            b_loads.append(local(source, bx.at[half, xl, rows], load_sem.at[3 + 2 * half + n]))
    barrier = pltpu.get_barrier_semaphore()

    def greet(device):
        pl.semaphore_signal(barrier, inc=1, device_id=device, device_id_type=MESH)

    def y_device(k):
        return (lax.rem(y + k, NY) * NX + xl, c, t)

    def dp_device(k):
        other = lax.rem(d + k, NX * NY)
        return other, (other, c, t)

    loop(1, NX * NY, lambda k: greet(dp_device(k)[1]))
    greet(partner)
    for k in range(NY):
        greet((lax.rem(y + k, NY) * NX + 1 - xl, c + 1 - 2 * xh, t))

    place = xl * NY + y

    def greet_column(k):
        zz = lax.rem(z + k, NZ)
        greet((d, zz * NX, t))
        greet((d, zz * NX + 1, t))

    loop(1, NZ, greet_column)
    greet(sibling)
    kv_load.start()
    q_load.start()
    do_load.start()
    for copy in b_loads:
        copy.start()

    def attend(j, diagonal=False):
        if not diagonal:
            same = docs_ref[0, c] == docs_ref[0, c - j]
            bias = jnp.where(same, 0.0, NEG).astype(F32)
        for g in range(2):
            columns = slice(g * HEAD, (g + 1) * HEAD)
            s = dot(kvg[j, 0, :, columns], qt[g]) * INV_ROOT
            if diagonal:
                rows = lax.broadcasted_iota(jnp.int32, s.shape, 0)
                lanes = lax.broadcasted_iota(jnp.int32, s.shape, 1) & (BLOCK - 1)
                s = jnp.where(rows <= lanes, s, NEG)
                top = jnp.max(s, axis=0, keepdims=True)
            else:
                s = s + bias
                top = jnp.maximum(mx[g], jnp.max(s, axis=0, keepdims=True))
            p = jnp.exp(s - top)
            w[j, g] = p
            at[j, g] = top
            term = dot(kvg[j, 1, :, columns], p.astype(BF16), ((0,), (0,)))
            total = jnp.sum(p, axis=0, keepdims=True)
            if not diagonal:
                factor = jnp.exp(mx[g] - top)
                term += ot[g] * factor
                total += den[g] * factor
            mx[g] = top
            ot[g] = term
            den[g] = total

    pl.semaphore_wait(barrier, (NX * NY - 1) + 1 + NY + 2 * (NZ - 1) + 1)

    def forward_kv(s, h):
        slot = 2 * s

        def to(dst, send, device):
            remote(kvg.at[slot, h], kvg.at[dst, h], send, kv_recv.at[dst, h], device).start()

        @pl.when((s <= 3) & (z <= NZ - 2))
        def _():
            to(slot + 2, kv_send_z.at[s, h], above)

        @pl.when(xh == 0)
        def _():
            to(slot + 1, kv_send_x.at[s, h], partner)

        @pl.when((xh == 1) & (s >= 1))
        def _():
            to(slot - 1, kv_send_x.at[s, h], partner)

        @pl.when((xh == 1) & (s == 4) & (z <= NZ - 2))
        def _():
            to(9, kv_send_9.at[h], (d, c + 1, t))

    kv_load.wait()
    forward_kv(0, 0)
    forward_kv(0, 1)

    x_pair = (d + 1 - 2 * xl, c, t)
    x_other = (d + 1 - 2 * xl, c + 1 - 2 * xh, t)
    owners = [owner_ref[m] for m in range(4)]
    bx_copies = []
    for half, device in enumerate((x_pair, x_other)):
        for n, (source, rows) in enumerate(zip(mine_of(half), (pl.ds(0, 256), pl.ds(256, 32)))):
            bx_copies.append(
                remote(source, bx.at[half, xl, rows], bx_send.at[half, n], bx_recv.at[half, n], device)
            )
    for copy in bx_copies:
        copy.start()

    def send_inputs(steps):
        for core, source in enumerate((x_ref, gl_ref)):
            @pl.when(t == core)
            def _():
                for dy, dx in steps:
                    row = lax.rem(y + dy, NY)
                    other = row * NX + side(dx)
                    part = source.at[0, :, pl.ds(pl.multiple_of(other * 1024, 1024), 1024)]
                    send = a_send.at[dy * NX + dx]
                    if dy == dx == 0:
                        local(part, xr.at[core, place], load_sem.at[7]).start()
                    elif dy == 0:
                        remote(part, xr.at[core, place], send, a_recv.at[place], (x_pair, x_other)[core]).start()
                    elif dx == 0:
                        remote(part, xr.at[core, place], send, a_recv.at[place], y_device(dy)).start()
                    else:
                        remote(part, relay.at[y], send, relay_recv.at[y], y_device(dy)).start()

    crossing = (d + 1 - 2 * xl, c + t * (1 - 2 * xh), t)

    def relay_copy(k):
        row = lax.rem(y + k, NY)
        slot = xl * NY + row
        return remote(relay.at[row], xr.at[t, slot], relay_send.at[row], a_recv.at[slot], crossing)

    def relay_on(k):
        row = lax.rem(y + k, NY)
        arrived(relay.at[row], relay_recv.at[row])
        relay_copy(k).start()

    def side(dx):
        return xl if dx == 0 else 1 - xl

    send_inputs(((1, 0), (3, 0), (0, 0), (1, 1), (3, 1)))

    def split_heads(h):
        g, i = lax.div(h, 8), lax.rem(h, 8)
        columns = pl.ds(pl.multiple_of(h * HEAD, HEAD), HEAD)
        rows = pl.ds(pl.multiple_of(i * HEAD, HEAD), HEAD)
        tile = qf[:, columns]
        qs[g, rows, :] = tile
        qt[g, :, rows] = tile.T
        tile = dof[:, columns]
        dos[g, rows, :] = tile
        dot_[g, :, rows] = tile.T

    q_load.wait()
    do_load.wait()
    loop(0, 16, split_heads)
    attend(0, True)

    by_copies = [
        remote(pk.at[odd if k == 2 else 1 - odd], by.at[y], by_send.at[k], by_recv.at[y], y_device(k))
        for k in range(1, NY)
    ]

    def pick_x():
        for copy in b_loads:
            copy.wait()
        for copy in bx_copies:
            copy.wait_recv()
        for half, (wide, narrow) in enumerate(((0, 1), (3, 2))):
            pk[half, 0:256] = bx[half, lax.rem(owners[wide], NX), 0:256]
            pk[half, 256:288] = bx[half, lax.rem(owners[narrow], NX), 256:288]
        for copy in by_copies:
            copy.start()

    def pick_y():
        by[y] = pk[odd]
        for k in range(1, NY):
            yy = lax.rem(y + k, NY)
            arrived(by.at[yy], by_recv.at[yy])
        wide = jnp.where(odd == 0, owners[0], owners[3])
        narrow = jnp.where(odd == 0, owners[1], owners[2])
        bas[odd, z, 0:256] = by[lax.div(wide, NX), 0:256]
        bas[odd, z, 256:288] = by[lax.div(narrow, NX), 256:288]

    z_up = (d, lax.rem(z + 1, NZ) * NX + xh, t)
    z_down = (d, lax.rem(z + NZ - 1, NZ) * NX + xh, t)
    LOW, HIGH = pl.ds(0, 144), pl.ds(144, 144)

    def part_of(p):
        return lax.rem(p + 2 * NZ, NZ)

    def ring_parts(k, ways):
        parts = []
        for way, device, p in ways:
            ref = bas.at[odd, part_of(p)]
            if k == 3:
                ref = ref.at[(LOW, HIGH)[way]]
            parts.append((ref, ring_send.at[way, k], ring_recv.at[way, k], device))
        return parts

    def ring_copies(k):
        parts = ring_parts(k, ((0, z_up, z - k), (1, z_down, z + k)))
        return [remote(ref, ref, send, recv, device) for ref, send, recv, device in parts]

    def y_forward(p):
        p = part_of(p)
        return [
            remote(ref, ref, yf_send.at[n, p], yf_recv.at[n, p], y_device(k))
            for n, (ref, k) in enumerate(((bas.at[odd, p, LOW], 1), (bas.at[odd, p, HIGH], 3)))
        ]

    def ring_step(k):
        if k >= 1:
            for ref, _, recv, _ in ring_parts(k - 1, ((0, z_up, z - k), (1, z_down, z + k))):
                arrived(ref, recv)
        if k <= 3:
            for copy in ring_copies(k):
                copy.start()
        for p in ((z - k, z + k) if 1 <= k <= 3 else (z + k,)):
            for copy in y_forward(p):
                copy.start()

    def odd_slot(j):
        arrived(kvg.at[j, 0], kv_recv.at[j, 0])
        arrived(kvg.at[j, 1], kv_recv.at[j, 1])
        attend(j)

    def forward_step(s):
        @pl.when(z >= s)
        def _():
            arrived(kvg.at[2 * s, 0], kv_recv.at[2 * s, 0])
            forward_kv(s, 0)
            arrived(kvg.at[2 * s, 1], kv_recv.at[2 * s, 1])
            forward_kv(s, 1)
            attend(2 * s)

        @pl.when((s >= 2) & (z + xh >= s - 1))
        def _():
            odd_slot(2 * s - 3)

        @pl.when(s == 2)
        def _():
            pick_x()

    loop(1, 5, forward_step)
    pick_y()
    ring_step(0)

    def last_slots(s):
        @pl.when(z + xh >= s)
        def _():
            odd_slot(2 * s - 1)

    loop(4, 6, last_slots)

    send_inputs(((0, 1), (2, 0), (2, 1)))

    dqt[...] = jnp.zeros_like(dqt)
    for g in range(2):
        den[g] = 1.0 / den[g]
        low = (ot[g] * den[g]).astype(BF16)
        otl[g] = low
        delta[g] = jnp.sum(low.astype(F32) * dot_[g].astype(F32), axis=0, keepdims=True)

    def scale(j):
        for g in range(2):
            at[j, g] = jnp.exp(at[j, g] - mx[g]) * den[g]

    loop(0, jnp.minimum(c, LONGEST - 1) + 1, scale)
    ring_step(1)

    def backward(j, store):
        for g in range(2):
            columns = slice(g * HEAD, (g + 1) * HEAD)
            key = kvg[j, 0, :, columns]
            value = kvg[j, 1, :, columns]
            p = w[j, g] * at[j, g]
            ds = (p * (dot(value, dot_[g]) - delta[g])).astype(BF16)
            dqt[g] += dot(key, ds, ((0,), (0,)))
            store(0, columns, dot(ds, qs[g]) * INV_ROOT)
            store(1, columns, dot(p.astype(BF16), dos[g]))

    def chain(s):
        @pl.when(z >= s)
        def _():
            @pl.when((xh == 0) | (s >= 1))
            def _():
                arrived(xrecv.at[s], x_recv.at[s])
                dacc[s] += xrecv[s].astype(F32)

            @pl.when((s == 4) & (xh == 1) & (z <= NZ - 2))
            def _():
                arrived(ext, ext_recv.at[0])
                dacc[s] += ext[...].astype(F32)

            for h in range(2):
                @pl.when((s <= 3) & (z <= NZ - 2))
                def _():
                    arrived(tin.at[s, h], t_recv.at[s, h])
                    dacc[s, h] += tin[s, h].astype(F32)

                @pl.when(s >= 1)
                def _():
                    dsend[2 * s, h] = dacc[s, h].astype(BF16)
                    remote(
                        dsend.at[2 * s, h], tin.at[s - 1, h], t_send.at[s, h], t_recv.at[s - 1, h], below
                    ).start()

    def backward_step(i):
        s = 4 - i

        @pl.when(z + xh >= s + 1)
        def _():
            def store(which, columns, val):
                dsend[2 * s + 1, which, :, columns] = val.astype(BF16)

            backward(2 * s + 1, store)

            @pl.when(xh == 1)
            def _():
                remote(dsend.at[2 * s + 1], xrecv.at[s], x_send.at[s], x_recv.at[s], partner).start()

            @pl.when((xh == 0) & (s <= 3))
            def _():
                remote(dsend.at[2 * s + 1], xrecv.at[s + 1], x_send.at[s], x_recv.at[s + 1], partner).start()

            @pl.when((xh == 0) & (s == 4))
            def _():
                remote(dsend.at[9], ext, ext_send.at[0], ext_recv.at[0], (d, c - 1, t)).start()

        @pl.when(z >= s)
        def _():
            def store(which, columns, val):
                dacc[s, which, :, columns] = val

            backward(2 * s, store)

        @pl.when(i == 1)
        def _():
            ring_step(2)

        @pl.when(i == 2)
        def _():
            relay_on(1)

        @pl.when(i == 3)
        def _():
            ring_step(3)

    loop(0, 5, backward_step)
    relay_on(3)
    ring_step(4)
    chain(4)
    relay_on(2)

    def finish_grads(h):
        g, i = lax.div(h, 8), lax.rem(h, 8)
        columns = pl.ds(pl.multiple_of(h * HEAD, HEAD), HEAD)
        rows = pl.ds(pl.multiple_of(i * HEAD, HEAD), HEAD)
        gq_out[0, :, columns] = (dqt[g, :, rows] * INV_ROOT).astype(BF16).T
        att_out[0, :, columns] = otl[g, :, rows].T

    loop(0, 16, finish_grads)
    chain(3)
    hand_overs = [
        remote(ref, ref, sib_send.at[n], sib_recv.at[n], sibling)
        for n, ref in ((0, xr.at[t, pl.ds(xl * NY, NY)]), (4, xr.at[t, pl.ds((1 - xl) * NY, NY)]))
    ]

    def inputs_arrived(dx):
        for k in range(NY):
            at_y = side(dx) * NY + lax.rem(y + k, NY)
            if dx == 0 and k == 0:
                local(xr.at[t, place], xr.at[t, place], load_sem.at[7]).wait()
            else:
                arrived(xr.at[t, at_y], a_recv.at[at_y])
        hand_overs[dx].start()

    def other_arrived(dx):
        arrived(xr.at[1 - t, pl.ds(side(dx) * NY, NY)], sib_recv.at[4 * dx])

    def turn_piece(a, other):
        tokens = pl.ds(pl.multiple_of(other * 128, 128), 128)

        def one(group):
            for m in range(4):
                rows = pl.ds(pl.multiple_of(group * 512 + m * 128, 128), 128)
                xt[a, rows, tokens] = xr[a, other, :, rows].T

        loop(0, 2, one)

    def turn(a, dx):
        loop(0, NY, lambda n: turn_piece(a, side(dx) * NY + n))

    inputs_arrived(0)
    chain(2)
    turn(t, 0)

    for n in range(2):
        for p in range(NZ):
            arrived(bas.at[1 - odd, p, (LOW, HIGH)[n]], yf_recv.at[n, p])

    low_half = pl.ds(pl.multiple_of(t * 128, 128), 128)
    high_half = pl.ds(pl.multiple_of((1 - t) * 128, 128), 128)

    def give(part, pairs):
        for n, (rows, basis) in enumerate(pairs):
            pm[part, n] = dot(rows, basis)
            sx[part, n] = pm[part, n, :, high_half].astype(BF16)
        copy = remote(sx.at[part], rx.at[part], sib_send.at[1 + part], sib_recv.at[1 + part], sibling)
        copy.start()
        return copy

    def m_pieces(part):
        pieces = []
        for dx in range(NX):
            for k in range(NY):
                if dx == k == 0:
                    continue
                row = lax.rem(y + k, NY)
                other = row * NX + side(dx)
                slot = side(dx) * NY + row
                if dx == 0 or part == 1:
                    pieces.append((other, c, slot, dx * NY + k, 0, pl.ds(0, 256)))
                else:
                    pieces.append((other, c + 1 - 2 * xh, slot, dx * NY + k, 0, pl.ds(0, 128)))
                    pieces.append((other, c, slot, dx * NY + k, 1, pl.ds(128, 128)))
        return pieces

    def m_copies(part):
        copies = []
        for other, column, _, at_send, n, lanes in m_pieces(part):
            ref = mm.at[part, place, :, lanes]
            copies.append(
                remote(ref, ref, m_send.at[part, at_send, n], m_recv.at[part, place, n], (other, column, t))
            )
        return copies

    def m_arrived(part):
        for _, _, slot, _, n, lanes in m_pieces(part):
            arrived(mm.at[part, slot, :, lanes], m_recv.at[part, slot, n])

    def spread(part):
        arrived(rx.at[part], sib_recv.at[1 + part])
        for n in range(2):
            share = pm[part, n, :, low_half] + rx[part, n].astype(F32)
            mm[part, place, :, n * 128:(n + 1) * 128] = share.astype(BF16)
        for copy in m_copies(part):
            copy.start()

    def wide_basis(half):
        return bas[half, :, 0:256, :].reshape(NZ * 256, 256)

    def narrow_basis(half):
        return bas[half, :, 256:288, :].reshape(NZ * 32, 256)

    give_a = give(0, ((att_out[0], wide_basis(1)), (gq_out[0], wide_basis(0))))
    chain(1)
    spread(0)
    other_arrived(0)
    turn(1 - t, 0)

    chain(0)
    for h in range(2):
        gkv_out[h, 0] = dacc[0, h].astype(BF16)
    give_b = give(1, ((gkv_out[0, 0], narrow_basis(0)), (gkv_out[1, 0], narrow_basis(1))))
    spread(1)

    def x_copy(part):
        return remote(rs.at[part, 1 - xh], rr.at[part], r_send.at[part], r_recv.at[part], partner)

    def outer(part):
        tokens = NX * NY * 128

        def one(n):
            rows = pl.ds(pl.multiple_of(n * 256, 256), 256)
            if part == 0:
                out = dot(xt[1, rows, :], mm[0, :, :, 0:128].reshape(tokens, 128))
                gq = dot(xt[0, rows, :], mm[0, :, :, 128:256].reshape(tokens, 128))
                val = jnp.concatenate([out, gq], axis=1).astype(BF16)
            else:
                val = dot(xt[0, rows, :], mm[1].reshape(tokens, 256)).astype(BF16)
            for m in range(2):
                rs[part, 0, 2 * n + m] = val[m * 128:m * 128 + 64]
                rs[part, 1, 2 * n + m] = val[m * 128 + 64:m * 128 + 128]

        loop(0, NZ // 2, one)
        x_copy(part).start()

    def z_copy(part, k):
        zz = lax.rem(z + k, NZ)
        return remote(
            rs2.at[part, zz], rr2.at[part, z], z_send.at[part, k], z_recv.at[part, z], (d, zz * NX + xh, t)
        )

    def over_x(part):
        arrived(rr.at[part], r_recv.at[part])

        def one(zz):
            total = rs[part, xh, zz].astype(F32) + rr[part, zz].astype(F32)
            rs2[part, zz] = total.astype(BF16)

        loop(0, NZ, one)
        loop(1, NZ, lambda k: z_copy(part, k).start())

    def over_z(part, places):
        def one(k):
            zz = lax.rem(z + k, NZ)
            arrived(rr2.at[part, zz], z_recv.at[part, zz])

        loop(1, NZ, one)
        total = rs2[part, z].astype(F32)
        for k in range(1, NZ):
            total += rr2[part, lax.rem(z + k, NZ)].astype(F32)
        for n, m in enumerate(places):
            proj_out[:, m, :] = total[:, n * 128:(n + 1) * 128] * rssq[m:m + 1, low_half]

    def piece(k):
        return (1 - xl) * NY + lax.rem(y + k, NY)

    def piece_copy(k):
        ref = xr.at[t, piece(k)]
        return remote(ref, ref, piece_send.at[k], piece_recv.at[k], sibling)

    order = (0, 1, 3, 2)
    for k in order:
        arrived(xr.at[t, piece(k)], a_recv.at[piece(k)])
        piece_copy(k).start()
        turn_piece(t, piece(k))
    for k in order:
        arrived(xr.at[1 - t, piece(k)], piece_recv.at[k])
        turn_piece(1 - t, piece(k))
    m_arrived(0)
    outer(0)
    m_arrived(1)
    outer(1)
    for m, value in enumerate((wide_basis(0), narrow_basis(0), narrow_basis(1), wide_basis(1))):
        wide = value.astype(F32)
        ssq[m:m + 1, :] = jnp.sum(wide * wide, axis=0, keepdims=True)
    give_s = remote(ssq, rssq, sib_send.at[3], sib_recv.at[3], sibling)
    give_s.start()


    over_x(0)
    arrived(rssq, sib_recv.at[3])
    rssq[...] = lax.rsqrt(ssq[...] + rssq[...] + 1e-06) * (1.0 / 128.0)
    over_x(1)
    over_z(0, (3, 0))
    over_z(1, (1, 2))

    def kv_left(s):
        for h in range(2):
            @pl.when((z >= s) & (s <= 3) & (z <= NZ - 2))
            def _():
                left(kvg.at[0, h], kv_send_z.at[s, h])

            @pl.when((z >= s) & ((xh == 0) | (s >= 1)))
            def _():
                left(kvg.at[0, h], kv_send_x.at[s, h])

            @pl.when((z >= s) & (s >= 1))
            def _():
                left(dsend.at[0, h], t_send.at[s, h])

        @pl.when((z + xh >= s + 1) & ((xh == 1) | (s <= 3)))
        def _():
            left(dsend.at[0], x_send.at[s])

    loop(0, 5, kv_left)

    @pl.when((xh == 1) & (z >= 4) & (z <= NZ - 2))
    def _():
        for h in range(2):
            left(kvg.at[0, h], kv_send_9.at[h])

    @pl.when((xh == 0) & (z >= 5))
    def _():
        left(dsend.at[0], ext_send.at[0])

    for copy in bx_copies + by_copies:
        copy.wait_send()
    for k in range(4):
        for copy in ring_copies(k):
            copy.wait_send()
    for n in range(2):
        for p in range(NZ):
            left(bas.at[0, 0, LOW], yf_send.at[n, p])
    def dp_left(k):
        left(xr.at[0, 0], a_send.at[k])

    loop(1, NX * NY, dp_left)
    for part in range(2):
        x_copy(part).wait_send()
        for copy in m_copies(part):
            copy.wait_send()
    for k in range(1, NY):
        relay_copy(k).wait_send()
    for part in range(2):
        loop(1, NZ, lambda k: z_copy(part, k).wait_send())
    for k in range(NY):
        piece_copy(k).wait_send()
    for copy in (hand_overs[0], give_a, give_b, give_s):
        copy.wait_send()


def on_device(*args):
    dma = pltpu.SemaphoreType.DMA
    vmem = pltpu.VMEM
    scratch = [
        vmem((128, 2048), BF16), vmem((128, 2048), BF16),
        vmem((2, 1024, 128), BF16), vmem((2, 1024, 128), BF16),
        vmem((2, 128, 1024), BF16), vmem((2, 128, 1024), BF16),
        vmem((LONGEST, 2, 128, 256), BF16),
        vmem((LONGEST, 2, 128, 1024), F32),
        vmem((2, 1, 1024), F32), vmem((LONGEST, 2, 1, 1024), F32), vmem((2, 1, 1024), F32), vmem((2, 1, 1024), F32),
        vmem((2, 128, 1024), F32), vmem((2, 128, 1024), BF16), vmem((2, 128, 1024), F32),
        vmem((LONGEST, 2, 128, 256), BF16), vmem((5, 2, 128, 256), F32),
        vmem((5, 2, 128, 256), BF16), vmem((4, 2, 128, 256), BF16),
        vmem((2, 128, 256), BF16),
        vmem((2, 2, 288, 256), BF16), vmem((2, 288, 256), BF16), vmem((4, 288, 256), BF16),
        vmem((2, NZ, 288, 256), BF16),
        vmem((NY, 128, 1024), BF16), vmem((2, NX * NY, 128, 1024), BF16), vmem((2, 1024, NX * NY * 128), BF16),
        vmem((2, 2, 128, 256), F32), vmem((2, 2, 128, 128), BF16), vmem((2, 2, 128, 128), BF16),
        vmem((2, NX * NY, 128, 256), BF16),
        vmem((2, NX, NZ, 64, 256), BF16), vmem((2, NZ, 64, 256), BF16),
        vmem((2, NZ, 64, 256), BF16), vmem((2, NZ, 64, 256), BF16),
        vmem((4, 256), F32), vmem((4, 256), F32),
        dma((8,)),
        dma((10, 2)), dma((4, 2)), dma((5, 2)), dma((2,)),
        dma((5,)), dma((5,)), dma((5, 2)), dma((4, 2)), dma((1,)), dma((1,)),
        dma((2, 2)), dma((2, 2)), dma((4,)), dma((4,)), dma((2, 4)), dma((2, 4)), dma((2, NZ)), dma((2, NZ)),
        dma((NX * NY,)), dma((NX * NY,)), dma((NY,)), dma((NY,)), dma((NY,)), dma((NY,)), dma((5,)), dma((5,)),
        dma((2, NX * NY, 2)), dma((2, NX * NY, 2)), dma((2,)), dma((2,)), dma((2, NZ)), dma((2, NZ)),
    ]
    hbm = pl.BlockSpec(memory_space=pl.ANY)
    smem = pl.BlockSpec(memory_space=pltpu.SMEM)
    return pl.pallas_call(
        kernel,
        out_shape=(
            pltpu.VMEM((1, 128, 2048), BF16),
            pltpu.VMEM((1, 128, 2048), BF16),
            pltpu.VMEM((2, 1, 128, 256), BF16),
            pltpu.VMEM((64, 4, 128), F32),
        ),
        in_specs=[hbm] * 5 + [smem] + [hbm] * 2 + [smem],
        out_specs=(pl.BlockSpec(memory_space=pltpu.VMEM),) * 4,
        scratch_shapes=scratch,
        compiler_params=pltpu.CompilerParams(
            collective_id=0, has_side_effects=True, vmem_limit_bytes=60 * 1024 * 1024
        ),
        cost_estimate=pl.CostEstimate(flops=7_000_000_000, bytes_accessed=12_000_000, transcendentals=3_000_000),
    )(*args)


def solution(mesh):
    return jax.shard_map(
        on_device,
        mesh=mesh,
        in_specs=(
            P("dp", "ctx", None),
            P("dp", "ctx", "tp"),
            P(None, "dp", "ctx", "tp"),
            P("dp", "ctx", "tp"),
            P("dp", "ctx", None),
            P("dp", None),
            P(None, "dp", None, None),
            P(None, "dp", None, None),
            P(),
        ),
        out_specs=(
            P("dp", "ctx", "tp"),
            P("dp", "ctx", "tp"),
            P(None, "dp", "ctx", "tp"),
            P(("dp", "ctx"), None, "tp"),
        ),
        check_vma=False,
    )
```

```python
import math

import jax
import jax.numpy as jnp
from jax import lax
from jax.experimental import pallas as pl
from jax.experimental.pallas import tpu as pltpu
from jax.sharding import PartitionSpec as P

HEAD = 128
BLOCK = 128
LONGEST = 10
NEG = -1e30
MESH = pl.DeviceIdType.MESH
BF16 = jnp.bfloat16
F32 = jnp.float32
INV_ROOT = 1.0 / math.sqrt(HEAD)

NX = 2
NY = 4
NZ = 8


def dot(a, b, dims=((1,), (0,))):
    return lax.dot_general(a, b, (dims, ((), ())), preferred_element_type=F32)


def kernel(
    x_ref, q_ref, kv_ref, do_ref, gl_ref, docs_ref, wide_ref, narrow_ref, owner_ref,
    att_out, gq_out, gkv_out, proj_out,
    qf, dof, qs, dos, qt, dot_, kvg, w, mx, at, den, delta, ot, otl, dqt,
    dsend, dacc, xrecv, tin, ext,
    bx, pk, by, bas, relay, xr, xt, pm, sx, rx, mm, rs, rr, rs2, rr2, ssq, rssq,
    load_sem,
    kv_recv, kv_send_z, kv_send_x, kv_send_9,
    x_send, x_recv, t_send, t_recv, ext_send, ext_recv,
    bx_send, bx_recv, by_send, by_recv, ring_send, ring_recv, yf_send, yf_recv,
    a_send, a_recv, relay_send, relay_recv, piece_send, piece_recv, sib_send, sib_recv, m_send, m_recv, r_send, r_recv, z_send, z_recv,
):
    d = lax.axis_index("dp")
    c = lax.axis_index("ctx")
    t = lax.axis_index("tp")
    y, xl = lax.div(d, NX), lax.rem(d, NX)
    z, xh = lax.div(c, NX), lax.rem(c, NX)
    odd = lax.rem(y, 2)
    partner = (d, c + 1 - 2 * xh, t)
    above = (d, c + NX, t)
    below = (d, c - NX, t)
    sibling = (d, c, 1 - t)

    def local(src, dst, sem):
        return pltpu.make_async_copy(src, dst, sem)

    def remote(src, dst, send, recv, device):
        return pltpu.make_async_remote_copy(
            src_ref=src, dst_ref=dst, send_sem=send, recv_sem=recv,
            device_id=device, device_id_type=MESH,
        )

    def arrived(dst, recv):
        remote(dst, dst, recv, recv, sibling).wait_recv()

    def left(src, send):
        remote(src, src, send, send, sibling).wait_send()

    def loop(low, high, body):
        def step(i, carry):
            body(i)
            return carry
        lax.fori_loop(low, high, step, 0)

    q_load = local(q_ref.at[0], qf, load_sem.at[0])
    do_load = local(do_ref.at[0], dof, load_sem.at[1])
    kv_load = local(kv_ref.at[:, 0], kvg.at[0], load_sem.at[2])

    def mine_of(half):
        return (
            wide_ref.at[half, 0, pl.ds(pl.multiple_of(t * 2048 + z * 256, 256), 256), :],
            narrow_ref.at[half, 0, pl.ds(pl.multiple_of(t * 256 + z * 32, 32), 32), :],
        )

    b_loads = []
    for half in range(2):
        for n, (source, rows) in enumerate(zip(mine_of(half), (pl.ds(0, 256), pl.ds(256, 32)))):
            b_loads.append(local(source, bx.at[half, xl, rows], load_sem.at[3 + 2 * half + n]))
    barrier = pltpu.get_barrier_semaphore()

    def greet(device):
        pl.semaphore_signal(barrier, inc=1, device_id=device, device_id_type=MESH)

    def y_device(k):
        return (lax.rem(y + k, NY) * NX + xl, c, t)

    def dp_device(k):
        other = lax.rem(d + k, NX * NY)
        return other, (other, c, t)

    loop(1, NX * NY, lambda k: greet(dp_device(k)[1]))
    greet(partner)
    for k in range(NY):
        greet((lax.rem(y + k, NY) * NX + 1 - xl, c + 1 - 2 * xh, t))

    place = xl * NY + y

    def greet_column(k):
        zz = lax.rem(z + k, NZ)
        greet((d, zz * NX, t))
        greet((d, zz * NX + 1, t))

    loop(1, NZ, greet_column)
    greet(sibling)
    kv_load.start()
    q_load.start()
    do_load.start()
    for copy in b_loads:
        copy.start()

    def attend(j, diagonal=False):
        if not diagonal:
            same = docs_ref[0, c] == docs_ref[0, c - j]
            bias = jnp.where(same, 0.0, NEG).astype(F32)
        for g in range(2):
            columns = slice(g * HEAD, (g + 1) * HEAD)
            s = dot(kvg[j, 0, :, columns], qt[g]) * INV_ROOT
            if diagonal:
                rows = lax.broadcasted_iota(jnp.int32, s.shape, 0)
                lanes = lax.broadcasted_iota(jnp.int32, s.shape, 1) & (BLOCK - 1)
                s = jnp.where(rows <= lanes, s, NEG)
                top = jnp.max(s, axis=0, keepdims=True)
            else:
                s = s + bias
                top = jnp.maximum(mx[g], jnp.max(s, axis=0, keepdims=True))
            p = jnp.exp(s - top)
            w[j, g] = p
            at[j, g] = top
            term = dot(kvg[j, 1, :, columns], p.astype(BF16), ((0,), (0,)))
            total = jnp.sum(p, axis=0, keepdims=True)
            if not diagonal:
                factor = jnp.exp(mx[g] - top)
                term += ot[g] * factor
                total += den[g] * factor
            mx[g] = top
            ot[g] = term
            den[g] = total

    pl.semaphore_wait(barrier, (NX * NY - 1) + 1 + NY + 2 * (NZ - 1) + 1)

    def forward_kv(s, h):
        slot = 2 * s

        def to(dst, send, device):
            remote(kvg.at[slot, h], kvg.at[dst, h], send, kv_recv.at[dst, h], device).start()

        @pl.when((s <= 3) & (z <= NZ - 2))
        def _():
            to(slot + 2, kv_send_z.at[s, h], above)

        @pl.when(xh == 0)
        def _():
            to(slot + 1, kv_send_x.at[s, h], partner)

        @pl.when((xh == 1) & (s >= 1))
        def _():
            to(slot - 1, kv_send_x.at[s, h], partner)

        @pl.when((xh == 1) & (s == 4) & (z <= NZ - 2))
        def _():
            to(9, kv_send_9.at[h], (d, c + 1, t))

    kv_load.wait()
    forward_kv(0, 0)
    forward_kv(0, 1)

    x_pair = (d + 1 - 2 * xl, c, t)
    x_other = (d + 1 - 2 * xl, c + 1 - 2 * xh, t)
    owners = [owner_ref[m] for m in range(4)]
    bx_copies = []
    for half, device in enumerate((x_pair, x_other)):
        for n, (source, rows) in enumerate(zip(mine_of(half), (pl.ds(0, 256), pl.ds(256, 32)))):
            bx_copies.append(
                remote(source, bx.at[half, xl, rows], bx_send.at[half, n], bx_recv.at[half, n], device)
            )
    for copy in bx_copies:
        copy.start()

    def send_inputs(steps):
        for core, source in enumerate((x_ref, gl_ref)):
            @pl.when(t == core)
            def _():
                for dy, dx in steps:
                    row = lax.rem(y + dy, NY)
                    other = row * NX + side(dx)
                    part = source.at[0, :, pl.ds(pl.multiple_of(other * 1024, 1024), 1024)]
                    send = a_send.at[dy * NX + dx]
                    if dy == dx == 0:
                        local(part, xr.at[core, place], load_sem.at[7]).start()
                    elif dy == 0:
                        remote(part, xr.at[core, place], send, a_recv.at[place], (x_pair, x_other)[core]).start()
                    elif dx == 0:
                        remote(part, xr.at[core, place], send, a_recv.at[place], y_device(dy)).start()
                    else:
                        remote(part, relay.at[y], send, relay_recv.at[y], y_device(dy)).start()

    crossing = (d + 1 - 2 * xl, c + t * (1 - 2 * xh), t)

    def relay_copy(k):
        row = lax.rem(y + k, NY)
        slot = xl * NY + row
        return remote(relay.at[row], xr.at[t, slot], relay_send.at[row], a_recv.at[slot], crossing)

    def relay_on(k):
        row = lax.rem(y + k, NY)
        arrived(relay.at[row], relay_recv.at[row])
        relay_copy(k).start()

    def side(dx):
        return xl if dx == 0 else 1 - xl

    send_inputs(((1, 0), (3, 0), (0, 0)))

    def split_heads(h):
        g, i = lax.div(h, 8), lax.rem(h, 8)
        columns = pl.ds(pl.multiple_of(h * HEAD, HEAD), HEAD)
        rows = pl.ds(pl.multiple_of(i * HEAD, HEAD), HEAD)
        tile = qf[:, columns]
        qs[g, rows, :] = tile
        qt[g, :, rows] = tile.T
        tile = dof[:, columns]
        dos[g, rows, :] = tile
        dot_[g, :, rows] = tile.T

    q_load.wait()
    do_load.wait()
    loop(0, 16, split_heads)
    attend(0, True)

    by_copies = [
        remote(pk.at[odd if k == 2 else 1 - odd], by.at[y], by_send.at[k], by_recv.at[y], y_device(k))
        for k in range(1, NY)
    ]

    def pick_x():
        for copy in b_loads:
            copy.wait()
        for copy in bx_copies:
            copy.wait_recv()
        for half, (wide, narrow) in enumerate(((0, 1), (3, 2))):
            pk[half, 0:256] = bx[half, lax.rem(owners[wide], NX), 0:256]
            pk[half, 256:288] = bx[half, lax.rem(owners[narrow], NX), 256:288]
        for copy in by_copies:
            copy.start()

    def pick_y():
        by[y] = pk[odd]
        for k in range(1, NY):
            yy = lax.rem(y + k, NY)
            arrived(by.at[yy], by_recv.at[yy])
        wide = jnp.where(odd == 0, owners[0], owners[3])
        narrow = jnp.where(odd == 0, owners[1], owners[2])
        bas[odd, z, 0:256] = by[lax.div(wide, NX), 0:256]
        bas[odd, z, 256:288] = by[lax.div(narrow, NX), 256:288]

    z_up = (d, lax.rem(z + 1, NZ) * NX + xh, t)
    z_down = (d, lax.rem(z + NZ - 1, NZ) * NX + xh, t)
    LOW, HIGH = pl.ds(0, 144), pl.ds(144, 144)

    def part_of(p):
        return lax.rem(p + 2 * NZ, NZ)

    def ring_parts(k, ways):
        parts = []
        for way, device, p in ways:
            ref = bas.at[odd, part_of(p)]
            if k == 3:
                ref = ref.at[(LOW, HIGH)[way]]
            parts.append((ref, ring_send.at[way, k], ring_recv.at[way, k], device))
        return parts

    def ring_copies(k):
        parts = ring_parts(k, ((0, z_up, z - k), (1, z_down, z + k)))
        return [remote(ref, ref, send, recv, device) for ref, send, recv, device in parts]

    def y_forward(p):
        p = part_of(p)
        return [
            remote(ref, ref, yf_send.at[n, p], yf_recv.at[n, p], y_device(k))
            for n, (ref, k) in enumerate(((bas.at[odd, p, LOW], 1), (bas.at[odd, p, HIGH], 3)))
        ]

    def ring_step(k):
        if k >= 1:
            for ref, _, recv, _ in ring_parts(k - 1, ((0, z_up, z - k), (1, z_down, z + k))):
                arrived(ref, recv)
        if k <= 3:
            for copy in ring_copies(k):
                copy.start()
        for p in ((z - k, z + k) if 1 <= k <= 3 else (z + k,)):
            for copy in y_forward(p):
                copy.start()

    def odd_slot(j):
        arrived(kvg.at[j, 0], kv_recv.at[j, 0])
        arrived(kvg.at[j, 1], kv_recv.at[j, 1])
        attend(j)

    def forward_step(s):
        @pl.when(z >= s)
        def _():
            arrived(kvg.at[2 * s, 0], kv_recv.at[2 * s, 0])
            forward_kv(s, 0)
            arrived(kvg.at[2 * s, 1], kv_recv.at[2 * s, 1])
            forward_kv(s, 1)
            attend(2 * s)

        @pl.when((s >= 2) & (z + xh >= s - 1))
        def _():
            odd_slot(2 * s - 3)

        @pl.when(s == 2)
        def _():
            pick_x()
            send_inputs(((1, 1), (3, 1)))

    loop(1, 5, forward_step)
    pick_y()
    ring_step(0)

    def last_slots(s):
        @pl.when(z + xh >= s)
        def _():
            odd_slot(2 * s - 1)

    loop(4, 6, last_slots)

    send_inputs(((0, 1), (2, 0), (2, 1)))

    dqt[...] = jnp.zeros_like(dqt)
    for g in range(2):
        den[g] = 1.0 / den[g]
        low = (ot[g] * den[g]).astype(BF16)
        otl[g] = low
        delta[g] = jnp.sum(low.astype(F32) * dot_[g].astype(F32), axis=0, keepdims=True)

    def scale(j):
        for g in range(2):
            at[j, g] = jnp.exp(at[j, g] - mx[g]) * den[g]

    loop(0, jnp.minimum(c, LONGEST - 1) + 1, scale)
    ring_step(1)

    def backward(j, store):
        for g in range(2):
            columns = slice(g * HEAD, (g + 1) * HEAD)
            key = kvg[j, 0, :, columns]
            value = kvg[j, 1, :, columns]
            p = w[j, g] * at[j, g]
            ds = (p * (dot(value, dot_[g]) - delta[g])).astype(BF16)
            dqt[g] += dot(key, ds, ((0,), (0,)))
            store(0, columns, dot(ds, qs[g]) * INV_ROOT)
            store(1, columns, dot(p.astype(BF16), dos[g]))

    def chain(s):
        @pl.when(z >= s)
        def _():
            @pl.when((xh == 0) | (s >= 1))
            def _():
                arrived(xrecv.at[s], x_recv.at[s])
                dacc[s] += xrecv[s].astype(F32)

            @pl.when((s == 4) & (xh == 1) & (z <= NZ - 2))
            def _():
                arrived(ext, ext_recv.at[0])
                dacc[s] += ext[...].astype(F32)

            for h in range(2):
                @pl.when((s <= 3) & (z <= NZ - 2))
                def _():
                    arrived(tin.at[s, h], t_recv.at[s, h])
                    dacc[s, h] += tin[s, h].astype(F32)

                @pl.when(s >= 1)
                def _():
                    dsend[2 * s, h] = dacc[s, h].astype(BF16)
                    remote(
                        dsend.at[2 * s, h], tin.at[s - 1, h], t_send.at[s, h], t_recv.at[s - 1, h], below
                    ).start()

    def backward_step(i):
        s = 4 - i

        @pl.when(z + xh >= s + 1)
        def _():
            def store(which, columns, val):
                dsend[2 * s + 1, which, :, columns] = val.astype(BF16)

            backward(2 * s + 1, store)

            @pl.when(xh == 1)
            def _():
                remote(dsend.at[2 * s + 1], xrecv.at[s], x_send.at[s], x_recv.at[s], partner).start()

            @pl.when((xh == 0) & (s <= 3))
            def _():
                remote(dsend.at[2 * s + 1], xrecv.at[s + 1], x_send.at[s], x_recv.at[s + 1], partner).start()

            @pl.when((xh == 0) & (s == 4))
            def _():
                remote(dsend.at[9], ext, ext_send.at[0], ext_recv.at[0], (d, c - 1, t)).start()

        @pl.when(z >= s)
        def _():
            def store(which, columns, val):
                dacc[s, which, :, columns] = val

            backward(2 * s, store)

        @pl.when(i == 1)
        def _():
            ring_step(2)

        @pl.when(i == 2)
        def _():
            relay_on(1)

        @pl.when(i == 3)
        def _():
            ring_step(3)

    loop(0, 5, backward_step)
    relay_on(3)
    ring_step(4)
    chain(4)
    relay_on(2)

    def finish_grads(h):
        g, i = lax.div(h, 8), lax.rem(h, 8)
        columns = pl.ds(pl.multiple_of(h * HEAD, HEAD), HEAD)
        rows = pl.ds(pl.multiple_of(i * HEAD, HEAD), HEAD)
        gq_out[0, :, columns] = (dqt[g, :, rows] * INV_ROOT).astype(BF16).T
        att_out[0, :, columns] = otl[g, :, rows].T

    loop(0, 16, finish_grads)
    chain(3)
    hand_overs = [
        remote(ref, ref, sib_send.at[n], sib_recv.at[n], sibling)
        for n, ref in ((0, xr.at[t, pl.ds(xl * NY, NY)]), (4, xr.at[t, pl.ds((1 - xl) * NY, NY)]))
    ]

    def inputs_arrived(dx):
        for k in range(NY):
            at_y = side(dx) * NY + lax.rem(y + k, NY)
            if dx == 0 and k == 0:
                local(xr.at[t, place], xr.at[t, place], load_sem.at[7]).wait()
            else:
                arrived(xr.at[t, at_y], a_recv.at[at_y])
        hand_overs[dx].start()

    def other_arrived(dx):
        arrived(xr.at[1 - t, pl.ds(side(dx) * NY, NY)], sib_recv.at[4 * dx])

    def turn_piece(a, other):
        tokens = pl.ds(pl.multiple_of(other * 128, 128), 128)

        def one(group):
            for m in range(4):
                rows = pl.ds(pl.multiple_of(group * 512 + m * 128, 128), 128)
                xt[a, rows, tokens] = xr[a, other, :, rows].T

        loop(0, 2, one)

    def turn(a, dx):
        loop(0, NY, lambda n: turn_piece(a, side(dx) * NY + n))

    inputs_arrived(0)
    chain(2)
    turn(t, 0)

    for n in range(2):
        for p in range(NZ):
            arrived(bas.at[1 - odd, p, (LOW, HIGH)[n]], yf_recv.at[n, p])

    low_half = pl.ds(pl.multiple_of(t * 128, 128), 128)
    high_half = pl.ds(pl.multiple_of((1 - t) * 128, 128), 128)

    def give(part, pairs):
        for n, (rows, basis) in enumerate(pairs):
            pm[part, n] = dot(rows, basis)
            sx[part, n] = pm[part, n, :, high_half].astype(BF16)
        copy = remote(sx.at[part], rx.at[part], sib_send.at[1 + part], sib_recv.at[1 + part], sibling)
        copy.start()
        return copy

    def m_pieces(part):
        pieces = []
        for dx in range(NX):
            for k in range(NY):
                if dx == k == 0:
                    continue
                row = lax.rem(y + k, NY)
                other = row * NX + side(dx)
                slot = side(dx) * NY + row
                if dx == 0 or part == 1:
                    pieces.append((other, c, slot, dx * NY + k, 0, pl.ds(0, 256)))
                else:
                    pieces.append((other, c + 1 - 2 * xh, slot, dx * NY + k, 0, pl.ds(0, 128)))
                    pieces.append((other, c, slot, dx * NY + k, 1, pl.ds(128, 128)))
        return pieces

    def m_copies(part):
        copies = []
        for other, column, _, at_send, n, lanes in m_pieces(part):
            ref = mm.at[part, place, :, lanes]
            copies.append(
                remote(ref, ref, m_send.at[part, at_send, n], m_recv.at[part, place, n], (other, column, t))
            )
        return copies

    def m_arrived(part):
        for _, _, slot, _, n, lanes in m_pieces(part):
            arrived(mm.at[part, slot, :, lanes], m_recv.at[part, slot, n])

    def spread(part):
        arrived(rx.at[part], sib_recv.at[1 + part])
        for n in range(2):
            share = pm[part, n, :, low_half] + rx[part, n].astype(F32)
            mm[part, place, :, n * 128:(n + 1) * 128] = share.astype(BF16)
        for copy in m_copies(part):
            copy.start()

    def wide_basis(half):
        return bas[half, :, 0:256, :].reshape(NZ * 256, 256)

    def narrow_basis(half):
        return bas[half, :, 256:288, :].reshape(NZ * 32, 256)

    give_a = give(0, ((att_out[0], wide_basis(1)), (gq_out[0], wide_basis(0))))
    chain(1)
    spread(0)
    other_arrived(0)
    turn(1 - t, 0)

    chain(0)
    for h in range(2):
        gkv_out[h, 0] = dacc[0, h].astype(BF16)
    give_b = give(1, ((gkv_out[0, 0], narrow_basis(0)), (gkv_out[1, 0], narrow_basis(1))))
    spread(1)

    def x_copy(part):
        return remote(rs.at[part, 1 - xh], rr.at[part], r_send.at[part], r_recv.at[part], partner)

    def outer(part):
        tokens = NX * NY * 128

        def one(n):
            rows = pl.ds(pl.multiple_of(n * 256, 256), 256)
            if part == 0:
                out = dot(xt[1, rows, :], mm[0, :, :, 0:128].reshape(tokens, 128))
                gq = dot(xt[0, rows, :], mm[0, :, :, 128:256].reshape(tokens, 128))
                val = jnp.concatenate([out, gq], axis=1).astype(BF16)
            else:
                val = dot(xt[0, rows, :], mm[1].reshape(tokens, 256)).astype(BF16)
            for m in range(2):
                rs[part, 0, 2 * n + m] = val[m * 128:m * 128 + 64]
                rs[part, 1, 2 * n + m] = val[m * 128 + 64:m * 128 + 128]

        loop(0, NZ // 2, one)
        x_copy(part).start()

    def z_copy(part, k):
        zz = lax.rem(z + k, NZ)
        return remote(
            rs2.at[part, zz], rr2.at[part, z], z_send.at[part, k], z_recv.at[part, z], (d, zz * NX + xh, t)
        )

    def over_x(part):
        arrived(rr.at[part], r_recv.at[part])

        def one(zz):
            total = rs[part, xh, zz].astype(F32) + rr[part, zz].astype(F32)
            rs2[part, zz] = total.astype(BF16)

        loop(0, NZ, one)
        loop(1, NZ, lambda k: z_copy(part, k).start())

    def over_z(part, places):
        def one(k):
            zz = lax.rem(z + k, NZ)
            arrived(rr2.at[part, zz], z_recv.at[part, zz])

        loop(1, NZ, one)
        total = rs2[part, z].astype(F32)
        for k in range(1, NZ):
            total += rr2[part, lax.rem(z + k, NZ)].astype(F32)
        for n, m in enumerate(places):
            proj_out[:, m, :] = total[:, n * 128:(n + 1) * 128] * rssq[m:m + 1, low_half]

    def piece(k):
        return (1 - xl) * NY + lax.rem(y + k, NY)

    def piece_copy(k):
        ref = xr.at[t, piece(k)]
        return remote(ref, ref, piece_send.at[k], piece_recv.at[k], sibling)

    order = (0, 1, 3, 2)
    for k in order:
        arrived(xr.at[t, piece(k)], a_recv.at[piece(k)])
        piece_copy(k).start()
        turn_piece(t, piece(k))
    for k in order:
        arrived(xr.at[1 - t, piece(k)], piece_recv.at[k])
        turn_piece(1 - t, piece(k))
    m_arrived(0)
    outer(0)
    m_arrived(1)
    outer(1)
    for m, value in enumerate((wide_basis(0), narrow_basis(0), narrow_basis(1), wide_basis(1))):
        wide = value.astype(F32)
        ssq[m:m + 1, :] = jnp.sum(wide * wide, axis=0, keepdims=True)
    give_s = remote(ssq, rssq, sib_send.at[3], sib_recv.at[3], sibling)
    give_s.start()


    over_x(0)
    arrived(rssq, sib_recv.at[3])
    rssq[...] = lax.rsqrt(ssq[...] + rssq[...] + 1e-06) * (1.0 / 128.0)
    over_x(1)
    over_z(0, (3, 0))
    over_z(1, (1, 2))

    def kv_left(s):
        for h in range(2):
            @pl.when((z >= s) & (s <= 3) & (z <= NZ - 2))
            def _():
                left(kvg.at[0, h], kv_send_z.at[s, h])

            @pl.when((z >= s) & ((xh == 0) | (s >= 1)))
            def _():
                left(kvg.at[0, h], kv_send_x.at[s, h])

            @pl.when((z >= s) & (s >= 1))
            def _():
                left(dsend.at[0, h], t_send.at[s, h])

        @pl.when((z + xh >= s + 1) & ((xh == 1) | (s <= 3)))
        def _():
            left(dsend.at[0], x_send.at[s])

    loop(0, 5, kv_left)

    @pl.when((xh == 1) & (z >= 4) & (z <= NZ - 2))
    def _():
        for h in range(2):
            left(kvg.at[0, h], kv_send_9.at[h])

    @pl.when((xh == 0) & (z >= 5))
    def _():
        left(dsend.at[0], ext_send.at[0])

    for copy in bx_copies + by_copies:
        copy.wait_send()
    for k in range(4):
        for copy in ring_copies(k):
            copy.wait_send()
    for n in range(2):
        for p in range(NZ):
            left(bas.at[0, 0, LOW], yf_send.at[n, p])
    def dp_left(k):
        left(xr.at[0, 0], a_send.at[k])

    loop(1, NX * NY, dp_left)
    for part in range(2):
        x_copy(part).wait_send()
        for copy in m_copies(part):
            copy.wait_send()
    for k in range(1, NY):
        relay_copy(k).wait_send()
    for part in range(2):
        loop(1, NZ, lambda k: z_copy(part, k).wait_send())
    for k in range(NY):
        piece_copy(k).wait_send()
    for copy in (hand_overs[0], give_a, give_b, give_s):
        copy.wait_send()


def on_device(*args):
    dma = pltpu.SemaphoreType.DMA
    vmem = pltpu.VMEM
    scratch = [
        vmem((128, 2048), BF16), vmem((128, 2048), BF16),
        vmem((2, 1024, 128), BF16), vmem((2, 1024, 128), BF16),
        vmem((2, 128, 1024), BF16), vmem((2, 128, 1024), BF16),
        vmem((LONGEST, 2, 128, 256), BF16),
        vmem((LONGEST, 2, 128, 1024), F32),
        vmem((2, 1, 1024), F32), vmem((LONGEST, 2, 1, 1024), F32), vmem((2, 1, 1024), F32), vmem((2, 1, 1024), F32),
        vmem((2, 128, 1024), F32), vmem((2, 128, 1024), BF16), vmem((2, 128, 1024), F32),
        vmem((LONGEST, 2, 128, 256), BF16), vmem((5, 2, 128, 256), F32),
        vmem((5, 2, 128, 256), BF16), vmem((4, 2, 128, 256), BF16),
        vmem((2, 128, 256), BF16),
        vmem((2, 2, 288, 256), BF16), vmem((2, 288, 256), BF16), vmem((4, 288, 256), BF16),
        vmem((2, NZ, 288, 256), BF16),
        vmem((NY, 128, 1024), BF16), vmem((2, NX * NY, 128, 1024), BF16), vmem((2, 1024, NX * NY * 128), BF16),
        vmem((2, 2, 128, 256), F32), vmem((2, 2, 128, 128), BF16), vmem((2, 2, 128, 128), BF16),
        vmem((2, NX * NY, 128, 256), BF16),
        vmem((2, NX, NZ, 64, 256), BF16), vmem((2, NZ, 64, 256), BF16),
        vmem((2, NZ, 64, 256), BF16), vmem((2, NZ, 64, 256), BF16),
        vmem((4, 256), F32), vmem((4, 256), F32),
        dma((8,)),
        dma((10, 2)), dma((4, 2)), dma((5, 2)), dma((2,)),
        dma((5,)), dma((5,)), dma((5, 2)), dma((4, 2)), dma((1,)), dma((1,)),
        dma((2, 2)), dma((2, 2)), dma((4,)), dma((4,)), dma((2, 4)), dma((2, 4)), dma((2, NZ)), dma((2, NZ)),
        dma((NX * NY,)), dma((NX * NY,)), dma((NY,)), dma((NY,)), dma((NY,)), dma((NY,)), dma((5,)), dma((5,)),
        dma((2, NX * NY, 2)), dma((2, NX * NY, 2)), dma((2,)), dma((2,)), dma((2, NZ)), dma((2, NZ)),
    ]
    hbm = pl.BlockSpec(memory_space=pl.ANY)
    smem = pl.BlockSpec(memory_space=pltpu.SMEM)
    return pl.pallas_call(
        kernel,
        out_shape=(
            pltpu.VMEM((1, 128, 2048), BF16),
            pltpu.VMEM((1, 128, 2048), BF16),
            pltpu.VMEM((2, 1, 128, 256), BF16),
            pltpu.VMEM((64, 4, 128), F32),
        ),
        in_specs=[hbm] * 5 + [smem] + [hbm] * 2 + [smem],
        out_specs=(pl.BlockSpec(memory_space=pltpu.VMEM),) * 4,
        scratch_shapes=scratch,
        compiler_params=pltpu.CompilerParams(
            collective_id=0, has_side_effects=True, vmem_limit_bytes=60 * 1024 * 1024
        ),
        cost_estimate=pl.CostEstimate(flops=7_000_000_000, bytes_accessed=12_000_000, transcendentals=3_000_000),
    )(*args)


def solution(mesh):
    return jax.shard_map(
        on_device,
        mesh=mesh,
        in_specs=(
            P("dp", "ctx", None),
            P("dp", "ctx", "tp"),
            P(None, "dp", "ctx", "tp"),
            P("dp", "ctx", "tp"),
            P("dp", "ctx", None),
            P("dp", None),
            P(None, "dp", None, None),
            P(None, "dp", None, None),
            P(),
        ),
        out_specs=(
            P("dp", "ctx", "tp"),
            P("dp", "ctx", "tp"),
            P(None, "dp", "ctx", "tp"),
            P(("dp", "ctx"), None, "tp"),
        ),
        check_vma=False,
    )
```
